32 devices in a mesh: dp: 8 (over y, x, core), mp: 4 (over z).
Axes of the slice: x: 2, y: 2, z: 4, core: 2. Of those that a mesh axis runs over, the one named last changes fastest.
Arguments:
- hidden_in: bfloat16 [8192, 1024], P('dp'), may hold values from -6 to 6
- key_mask: int32 [8192], P('dp'), may hold values from 0 to 1, as said below
- bucket_of_offset: int32 [2047], replicated, may hold values from 0 to 511, as said below
- position_table: bfloat16 [512, 1024], replicated, may hold values from -6 to 6
- query_weight: bfloat16 [1024, 1024], P(None, 'mp'), may hold values from -0.1875 to 0.1875
- query_bias: bfloat16 [1024], P('mp'), may hold values from -3 to 3
- key_weight: bfloat16 [1024, 1024], P(None, 'mp'), may hold values from -0.1875 to 0.1875
- key_bias: bfloat16 [1024], P('mp'), may hold values from -3 to 3
- value_weight: bfloat16 [1024, 1024], P(None, 'mp'), may hold values from -0.1875 to 0.1875
- value_bias: bfloat16 [1024], P('mp'), may hold values from -3 to 3
- out_weight: bfloat16 [1024, 1024], P('mp'), may hold values from -3 to 3
- out_bias: bfloat16 [1024], replicated, may hold values from -3 to 3
- first_gain: bfloat16 [1024], replicated, may hold values from 0.5 to 1.5
- first_shift: bfloat16 [1024], replicated, may hold values from -1.75 to 1.75
- up_weight: bfloat16 [1024, 4096], P(None, 'mp'), may hold values from -0.1875 to 0.1875
- up_bias: bfloat16 [4096], P('mp'), may hold values from -3 to 3
- down_weight: bfloat16 [4096, 1024], P('mp'), may hold values from -0.09375 to 0.09375
- down_bias: bfloat16 [1024], replicated, may hold values from -3 to 3
- second_gain: bfloat16 [1024], replicated, may hold values from 0.5 to 1.5
- second_shift: bfloat16 [1024], replicated, may hold values from -1.75 to 1.75
- cotangent: bfloat16 [8192, 1024], P(('dp', 'mp')), may hold values from -6 to 6
Outputs:
- layer_out: bfloat16 [8192, 1024], P(('dp', 'mp'))
- input_grad: float32 [8192, 1024], P(('dp', 'mp'))
- table_grad: float32 [512, 1024], replicated
- query_weight_grad: float32 [1024, 1024], P(None, 'mp')
- query_bias_grad: float32 [1024], P('mp')
- key_weight_grad: float32 [1024, 1024], P(None, 'mp')
- key_bias_grad: float32 [1024], P('mp')
- value_weight_grad: float32 [1024, 1024], P(None, 'mp')
- value_bias_grad: float32 [1024], P('mp')
- out_weight_grad: float32 [1024, 1024], P('mp')
- out_bias_grad: float32 [1024], replicated
- first_gain_grad: float32 [1024], replicated
- first_shift_grad: float32 [1024], replicated
- up_weight_grad: float32 [1024, 4096], P(None, 'mp')
- up_bias_grad: float32 [4096], P('mp')
- down_weight_grad: float32 [4096, 1024], P('mp')
- down_bias_grad: float32 [1024], replicated
- second_gain_grad: float32 [1024], replicated
- second_shift_grad: float32 [1024], replicated
The draws below stay inside these ranges and needn't reach their ends.
Inputs may be any that keep to these rules, and one draw needn't show every extreme that they name: `bucket_of_offset`: entry 1023 + o is the bucket of the offset o = i - j from key j to query i: it is 256 + o for |o| < min(128, 256), and never falls as o rises, by 0 or 1 a step. `key_mask`: in each sequence of 1024 tokens the ones form a prefix of 512 tokens or more, and its last token is 0.
All inputs are finite; a program needn't handle non-finite values.
Results may differ from the reference program's by a relative error of at most 0.029.
Values may be sent and summed in bfloat16 or wider, within the bound.
No kernel may reach another device: no remote copies, remote signals or barrier semaphores. Data moves between devices by JAX's collectives and lax.ppermute only.
A program may use at most 256 MiB of HBM per device.

```python
import math
import jax
import jax.numpy as jnp
from jax import lax

D = 1024
HEADS = 16
HEAD = 64
FF = 4096
POS_BUCKETS = 256
LEN = 1024
TOKENS = 8192


def draw_key_mask(key, part):
    key = jax.random.fold_in(key, 11)
    seq_count = TOKENS // LEN
    lengths = jax.random.randint(key, (seq_count, 1), LEN // 2, LEN)
    live_keys = jnp.arange(LEN, dtype=jnp.int32)[None, :] < lengths
    return live_keys.astype(jnp.int32).reshape(TOKENS)


def draw_bucket_of_offset(key, part):
    key = jax.random.fold_in(key, 23)
    near_span = min(POS_BUCKETS // 2, LEN // 4)
    far_count = LEN - near_span
    up_key, down_key = jax.random.split(key)
    rise_steps = (jax.random.permutation(up_key, far_count) < POS_BUCKETS - near_span).astype(jnp.int32)
    fall_steps = (jax.random.permutation(down_key, far_count) < POS_BUCKETS - near_span + 1).astype(jnp.int32)
    ahead_side = jnp.concatenate([POS_BUCKETS + jnp.arange(near_span, dtype=jnp.int32), POS_BUCKETS + near_span - 1 + jnp.cumsum(rise_steps).astype(jnp.int32)])
    behind = jnp.concatenate([POS_BUCKETS - jnp.arange(1, near_span, dtype=jnp.int32), POS_BUCKETS - near_span + 1 - jnp.cumsum(fall_steps).astype(jnp.int32)])
    return jnp.concatenate([behind[::-1], ahead_side]).astype(jnp.int32)


def shard_levels(own_key, extent, cuts, low, high):
    level = 1.0
    for dim, parts in cuts:
        draws = jax.random.uniform(jax.random.fold_in(jax.random.fold_in(own_key, 6), dim), (parts,), jnp.float32, low / len(cuts), high / len(cuts))
        level = level * jnp.repeat(jnp.exp(draws), extent[dim] // parts).reshape((-1,) + (1,) * (len(extent) - 1 - dim))
    return level


def gaussian(rng, dims, spread, most, cuts=(), kind=jnp.bfloat16):
    array = spread * jax.random.normal(rng, dims, jnp.float32)
    if cuts:
        array = array * shard_levels(rng, dims, cuts, -0.22, 0.18)
    return jnp.clip(array, -most, most).astype(kind)


def setup_inputs(seed: int = 0) -> dict:
    key_of = jax.random.split(jax.random.key(seed), 22)
    return {
        "hidden_in": gaussian(key_of[0], (TOKENS, D), 1.0, 6.0, ((0, 8),)),
        "key_mask": draw_key_mask(jax.random.fold_in(key_of[21], 71), 0),
        "bucket_of_offset": draw_bucket_of_offset(jax.random.fold_in(key_of[21], 71), 0),
        "position_table": gaussian(key_of[3], (2 * POS_BUCKETS, D), 1.0, 6.0),
        "query_weight": gaussian(key_of[4], (D, D), D ** -0.5, 0.1875, ((1, 4),)),
        "query_bias": gaussian(key_of[5], (D,), 0.5, 3.0, ((0, 4),)),
        "key_weight": gaussian(key_of[6], (D, D), D ** -0.5, 0.1875, ((1, 4),)),
        "key_bias": gaussian(key_of[7], (D,), 0.5, 3.0, ((0, 4),)),
        "value_weight": gaussian(key_of[8], (D, D), D ** -0.5, 0.1875, ((1, 4),)),
        "value_bias": gaussian(key_of[9], (D,), 0.5, 3.0, ((0, 4),)),
        "out_weight": gaussian(key_of[10], (D, D), (max(1, D // 256)) ** -0.5, 3.0, ((0, 4),)),
        "out_bias": gaussian(key_of[11], (D,), 0.5, 3.0),
        "first_gain": jnp.clip(1.0 + 0.1 * jax.random.normal(key_of[12], (D,), jnp.float32), 0.5, 1.5).astype(jnp.bfloat16),
        "first_shift": gaussian(key_of[13], (D,), 0.3, 1.75),
        "up_weight": gaussian(key_of[14], (D, FF), D ** -0.5, 0.1875, ((1, 4),)),
        "up_bias": gaussian(key_of[15], (FF,), 0.5, 3.0, ((0, 4),)),
        "down_weight": gaussian(key_of[16], (FF, D), FF ** -0.5, 0.09375, ((0, 4),)),
        "down_bias": gaussian(key_of[17], (D,), 0.5, 3.0),
        "second_gain": jnp.clip(1.0 + 0.1 * jax.random.normal(key_of[18], (D,), jnp.float32), 0.5, 1.5).astype(jnp.bfloat16),
        "second_shift": gaussian(key_of[19], (D,), 0.3, 1.75),
        "cotangent": gaussian(key_of[20], (TOKENS, D), 1.0, 6.0, ((0, 32),)),
    }


@jax.custom_vjp
def low(v):
    return lax.optimization_barrier(v.astype(jnp.bfloat16)).astype(jnp.float32)

@jax.custom_vjp
def low_back(v):
    return v

def low_keep(v):
    return (low(v), None)

def low_pass(kept, grad):
    return (grad,)

def back_keep(v):
    return (v, None)

def back_low(kept, grad):
    return (low(grad),)
low.defvjp(low_keep, low_pass)
low_back.defvjp(back_keep, back_low)
HIGHEST_PREC = lax.Precision.HIGHEST
NORM_EPS = 1e-07
MASK_FILL = -1000000000.0

def low_both(values):
    return low_back(low(values))

def matmul(left_arr, right_arr):
    return jnp.dot(left_arr, right_arr, precision=HIGHEST_PREC)

def norm_rows(values, gain_vec, shift_vec):
    row_mean = lax.optimization_barrier(jnp.mean(values, axis=-1, keepdims=True))
    centered = values - row_mean
    row_var = lax.optimization_barrier(jnp.mean(centered * centered, axis=-1, keepdims=True))
    return centered * lax.rsqrt(row_var + NORM_EPS) * gain_vec + shift_vec

def attention(queries, keys_all, values_all, pos_query, pos_key, bucket_of_offset, key_mask):
    tokens = queries.shape[0]
    blk_rows = min(512, LEN)
    per_seq = LEN // blk_rows
    step_count = tokens // LEN * per_seq
    score_scale = 1.0 / math.sqrt(3.0 * HEAD)

    def block_fn(step_at):
        seq_at = step_at // per_seq
        first_row = step_at % per_seq * blk_rows
        seq_base = seq_at * LEN
        q_blk = lax.dynamic_slice_in_dim(queries, seq_base + first_row, blk_rows, 0)
        k_seq = lax.dynamic_slice_in_dim(keys_all, seq_base, LEN, 0)
        v_seq = lax.dynamic_slice_in_dim(values_all, seq_base, LEN, 0)
        live_keys = lax.dynamic_slice_in_dim(key_mask, seq_base, LEN, 0)
        row_ids = first_row + jnp.arange(blk_rows, dtype=jnp.int32)
        col_ids = jnp.arange(LEN, dtype=jnp.int32)
        to_at = jnp.take(bucket_of_offset, row_ids[:, None] - col_ids[None, :] + LEN - 1)
        from_at = jnp.take(bucket_of_offset, col_ids[:, None] - row_ids[None, :] + LEN - 1)
        content = jnp.einsum('bhd,khd->hbk', q_blk, k_seq, precision=HIGHEST_PREC)
        near_q = jnp.einsum('bhd,rhd->hbr', q_blk, pos_key, precision=HIGHEST_PREC)
        to_pos = jnp.take_along_axis(near_q, jnp.broadcast_to(to_at[None], (HEADS, blk_rows, LEN)), axis=2)
        near_k = jnp.einsum('khd,rhd->hkr', k_seq, pos_query, precision=HIGHEST_PREC)
        from_pos = jnp.take_along_axis(near_k, jnp.broadcast_to(from_at[None], (HEADS, LEN, blk_rows)), axis=2)
        scores = low_back((content + to_pos + jnp.swapaxes(from_pos, 1, 2)) * score_scale)
        masked = jnp.where(live_keys[None, None, :] > 0, scores, MASK_FILL)
        row_max = lax.optimization_barrier(jnp.max(masked, axis=2, keepdims=True))
        exp_terms = jnp.exp(masked - row_max)
        attn_prob = low(exp_terms / lax.optimization_barrier(jnp.sum(exp_terms, axis=2, keepdims=True)))
        return jnp.einsum('hbk,khd->bhd', attn_prob, v_seq, precision=HIGHEST_PREC)
    output = lax.map(jax.checkpoint(block_fn), jnp.arange(step_count, dtype=jnp.int32))
    return output.reshape(tokens, HEADS * HEAD)

def layer_fwd(hidden_in, position_table, query_weight, query_bias, key_weight, key_bias, value_weight, value_bias, out_weight, out_bias, first_gain, first_shift, up_weight, up_bias, down_weight, down_bias, second_gain, second_shift, key_mask, bucket_of_offset):
    tokens = hidden_in.shape[0]
    queries = low_both(matmul(hidden_in, query_weight) + query_bias).reshape(tokens, HEADS, HEAD)
    keys_all = low_both(matmul(hidden_in, key_weight) + key_bias).reshape(tokens, HEADS, HEAD)
    values_all = low_both(matmul(hidden_in, value_weight) + value_bias).reshape(tokens, HEADS, HEAD)
    pos_query = low(matmul(position_table, query_weight) + query_bias).reshape(2 * POS_BUCKETS, HEADS, HEAD)
    pos_key = low(matmul(position_table, key_weight) + key_bias).reshape(2 * POS_BUCKETS, HEADS, HEAD)
    context = low_both(attention(queries, keys_all, values_all, pos_query, pos_key, bucket_of_offset, key_mask))
    attn_out = low_back(matmul(context, out_weight))
    normed = norm_rows(attn_out + out_bias + hidden_in, first_gain, first_shift)
    inner_pre = low_back(matmul(low(normed), up_weight) + up_bias)
    act_low = low(jax.nn.gelu(inner_pre, approximate=False))
    mixed = low_back(matmul(act_low, down_weight))
    return norm_rows(mixed + down_bias + normed, second_gain, second_shift)

def reference(hidden_in, key_mask, bucket_of_offset, position_table, query_weight, query_bias, key_weight, key_bias, value_weight, value_bias, out_weight, out_bias, first_gain, first_shift, up_weight, up_bias, down_weight, down_bias, second_gain, second_shift, cotangent):
    floats = [arr.astype(jnp.float32) for arr in (hidden_in, position_table, query_weight, query_bias, key_weight, key_bias, value_weight, value_bias, out_weight, out_bias, first_gain, first_shift, up_weight, up_bias, down_weight, down_bias, second_gain, second_shift)]

    def forward(*params):
        return layer_fwd(*params, key_mask, bucket_of_offset)
    output, pull_back = jax.vjp(forward, *floats)
    grad_all = pull_back(cotangent.astype(jnp.float32))
    return (output.astype(jnp.bfloat16), grad_all[0], grad_all[1], grad_all[2], grad_all[3], grad_all[4], grad_all[5], grad_all[6], grad_all[7], grad_all[8], grad_all[9], grad_all[10], grad_all[11], grad_all[12], grad_all[13], grad_all[14], grad_all[15], grad_all[16], grad_all[17])
```

```python
import math

import jax
import jax.numpy as jnp
from jax import lax
from jax.experimental import pallas as pl
from jax.experimental.pallas import tpu as pltpu
from jax.sharding import PartitionSpec as P

HEAD = 64
LEN = 1024


NORM_EPS = 1e-07
MASK_FILL = -1000000000.0


def norm_rows(values, gain_vec, shift_vec):
    row_mean = jnp.mean(values, axis=-1, keepdims=True)
    centered = values - row_mean
    row_var = jnp.mean(centered * centered, axis=-1, keepdims=True)
    return centered * lax.rsqrt(row_var + NORM_EPS) * gain_vec + shift_vec


def exact_gelu(values):
    return jax.nn.gelu(values, approximate=False)


def take_rows(values, start_at, row_count):
    return lax.dynamic_slice_in_dim(values, start_at, row_count, 0)


def add_rows(total_acc, part_rows, start_at):
    current = take_rows(total_acc, start_at, part_rows.shape[0])
    return lax.dynamic_update_slice_in_dim(total_acc, current + part_rows, start_at, 0)


def left_product(left_arr, right_arr):
    return lax.dot_general(
        left_arr, right_arr, (((0,), (0,)), ((), ())), preferred_element_type=jnp.float32
    )


def right_product(left_arr, right_arr):
    return lax.dot_general(
        left_arr, right_arr, (((1,), (1,)), ((), ())), preferred_element_type=jnp.float32
    )


def split_wide(values):
    upper_part = values.astype(jnp.bfloat16)
    lower_part = (values - upper_part.astype(jnp.float32)).astype(jnp.bfloat16)
    return (upper_part, lower_part)


def left_wide(narrow, wide_arr):
    upper_part, lower_part = split_wide(wide_arr)
    return left_product(narrow, upper_part) + left_product(narrow, lower_part)


def right_wide(wide_arr, narrow):
    upper_part, lower_part = split_wide(wide_arr)
    return right_product(upper_part, narrow) + right_product(lower_part, narrow)


NT=(((1,),(1,)),((),()))
NN=(((1,),(0,)),((),()))
TN=(((0,),(0,)),((),()))
def dot(a,b,dims):
    return lax.dot_general(a,b,dims,preferred_element_type=jnp.float32)
BLK=128
SCALE=1.0/math.sqrt(3.0*HEAD)

def half_of(x, half):
    lane=lax.broadcasted_iota(jnp.int32,(1,2*HEAD),1)
    return jnp.where((lane>=HEAD) if half else (lane<HEAD), x, jnp.zeros_like(x))

def eye(n):
    r=lax.broadcasted_iota(jnp.int32,(n,n),0); c=lax.broadcasted_iota(jnp.int32,(n,n),1)
    return (r==c).astype(jnp.float32).astype(jnp.bfloat16)

def shear(x):
    return pltpu.roll(x,0,1,stride=1,stride_axis=0)[:,BLK:]

def unshear(x, length):
    w=length+BLK
    x=jnp.concatenate([jnp.zeros((x.shape[0],BLK),x.dtype),x],axis=1)
    return pltpu.roll(x,0,1,stride=w-1,stride_axis=0)

def fwd_kernel(q_ref,k_ref,v_ref,kr_ref,qr_ref,mask_ref,p_ref,ctx_ref,f_scr):
    length=q_ref.shape[0]; nb=length//BLK; span=length+BLK
    def jb(b,_):
        j0=pl.multiple_of(b*BLK,BLK)
        slab=qr_ref[pl.ds(pl.multiple_of(length-BLK-j0,BLK),span),:]
        kb=k_ref[pl.ds(j0,BLK),:]
        for half in (0,1):
            g=dot(half_of(kb,half),slab,NT)
            f_scr[half,pl.ds(j0,BLK),:]=shear(g).astype(jnp.bfloat16)
        return 0
    lax.fori_loop(0,nb,jb,0)
    ident=eye(BLK)
    live=mask_ref[...]>0
    lane=lax.broadcasted_iota(jnp.int32,(1,2*HEAD),1)
    def ib(b,_):
        i0=pl.multiple_of(b*BLK,BLK)
        slab=kr_ref[pl.ds(pl.multiple_of(length-BLK-i0,BLK),span),:]
        qb=q_ref[pl.ds(i0,BLK),:]
        cs=[]
        for half in (0,1):
            qm=half_of(qb,half)
            t=shear(dot(qm,slab,NT))
            lhs=jnp.concatenate([ident,qm],axis=1)
            rhs=jnp.concatenate([f_scr[half,:,pl.ds(i0,BLK)],k_ref[...]],axis=1)
            s=(dot(lhs,rhs,NT)+t)*SCALE
            s=jnp.where(live,s,MASK_FILL)
            e=jnp.exp(s-jnp.max(s,axis=1,keepdims=True))
            p=(e*(1.0/jnp.sum(e,axis=1,keepdims=True))).astype(jnp.bfloat16)
            p_ref[half,pl.ds(i0,BLK),:]=p
            cs.append(dot(p,v_ref[...],NN))
        ctx_ref[pl.ds(i0,BLK),:]=jnp.where(lane<HEAD,cs[0],cs[1]).astype(jnp.bfloat16)
        return 0
    lax.fori_loop(0,nb,ib,0)

def attn_fwd(q,k,v,kr,qr,mask):
    length,width=q.shape
    pairs=width//(2*HEAD)
    col=pl.BlockSpec((length,2*HEAD),lambda g:(0,g))
    rows=pl.BlockSpec((2*length,2*HEAD),lambda g:(0,g))
    return pl.pallas_call(fwd_kernel,grid=(pairs,),
        in_specs=[col,col,col,rows,rows,pl.BlockSpec((1,length),lambda g:(0,0))],
        out_specs=[pl.BlockSpec((2,length,length),lambda g:(g,0,0)),col],
        out_shape=[jax.ShapeDtypeStruct((2*pairs,length,length),jnp.bfloat16),jax.ShapeDtypeStruct((length,width),jnp.bfloat16)],
        scratch_shapes=[pltpu.VMEM((2,length,length),jnp.bfloat16)],
        compiler_params=pltpu.CompilerParams(vmem_limit_bytes=56*2**20))(q,k,v,kr,qr,mask)

def flip(n):
    r=lax.broadcasted_iota(jnp.int32,(n,n),0); c=lax.broadcasted_iota(jnp.int32,(n,n),1)
    return (r+c==n-1).astype(jnp.float32).astype(jnp.bfloat16)

def spread(x, base):
    x=jnp.concatenate([x,jnp.zeros((x.shape[0],BLK),x.dtype)],axis=1)
    return pltpu.roll(x,base,1,stride=1,stride_axis=0)

def bwd_kernel(q_ref,k_ref,v_ref,kr_ref,qr_ref,p_ref,dc_ref,dq_ref,dk_ref,dv_ref,dkr_ref,dqr_ref,ds_scr,qrev_scr,dvt_scr,dkrt_scr,dqrt_scr):
    length=q_ref.shape[0]; nb=length//BLK; span=length+BLK
    lane=lax.broadcasted_iota(jnp.int32,(1,2*HEAD),1)
    ident=eye(BLK); rev=flip(BLK)
    bf=jnp.bfloat16
    dvt_scr[...]=jnp.zeros_like(dvt_scr)
    dkrt_scr[...]=jnp.zeros_like(dkrt_scr)
    dqrt_scr[...]=jnp.zeros_like(dqrt_scr)
    def ib(b,_):
        i0=pl.multiple_of(b*BLK,BLK)
        u0=pl.multiple_of(length-BLK-i0,BLK)
        slab=kr_ref[pl.ds(u0,span),:]
        qb=dot(rev,q_ref[pl.ds(i0,BLK),:],NN).astype(bf)
        qrev_scr[pl.ds(u0,BLK),:]=qb
        dcb=dc_ref[pl.ds(i0,BLK),:]
        dcr=dot(rev,dcb,NN).astype(bf)
        outs=[]; dvt=0; dkrt=0
        for half in (0,1):
            qm=half_of(qb,half)
            p=p_ref[half,pl.ds(i0,BLK),:]
            dp=dot(half_of(dcr,half),v_ref[...],NT)
            pr=dot(rev,p,NN)
            pd=pr*dp
            ds=pd-pr*jnp.sum(pd,axis=1,keepdims=True)
            dsl=ds.astype(bf)
            ds_scr[half,pl.ds(u0,BLK),:]=dsl
            dto=spread(ds,1).astype(bf)
            outs.append(dot(dsl,k_ref[...],NN)+dot(dto,slab,NN))
            dvt=dvt+dot(half_of(dcb,half),p,TN)
            dkrt=dkrt+dot(qm,dto,TN)
        dqb=(jnp.where(lane<HEAD,outs[0],outs[1])*SCALE).astype(bf)
        dq_ref[pl.ds(i0,BLK),:]=dot(rev,dqb,NN).astype(bf)
        dvt_scr[...]+=dvt
        dkrt_scr[:,pl.ds(u0,span)]+=dkrt
        return 0
    lax.fori_loop(0,nb,ib,0)
    def jb(b,_):
        j0=pl.multiple_of(b*BLK,BLK)
        slab=qr_ref[pl.ds(j0,span),:]
        kb=k_ref[pl.ds(j0,BLK),:]
        outs=[]; dqrt=0
        for half in (0,1):
            km=half_of(kb,half)
            dst=dot(ident,ds_scr[half,:,pl.ds(j0,BLK)],NT)
            dfrom=spread(dst,0).astype(bf)
            outs.append(dot(dst.astype(bf),qrev_scr[...],NN)+dot(dfrom,slab,NN))
            dqrt=dqrt+dot(km,dfrom,TN)
        dk_ref[pl.ds(j0,BLK),:]=(jnp.where(lane<HEAD,outs[0],outs[1])*SCALE).astype(bf)
        dqrt_scr[:,pl.ds(j0,span)]+=dqrt
        return 0
    lax.fori_loop(0,nb,jb,0)
    dv_ref[...]=dvt_scr[...].T.astype(bf)
    dkr_ref[...]=dkrt_scr[...]*SCALE
    dqr_ref[...]=dqrt_scr[...]*SCALE

def attn_bwd(q,k,v,kr,qr,p,dc):
    length,width=q.shape
    pairs=width//(2*HEAD)
    col=pl.BlockSpec((length,2*HEAD),lambda g:(0,g))
    rows=pl.BlockSpec((2*length,2*HEAD),lambda g:(0,g))
    rowst=pl.BlockSpec((2*HEAD,2*length),lambda g:(g,0))
    f32=jnp.float32
    cs=jax.ShapeDtypeStruct((length,width),jnp.bfloat16)
    return pl.pallas_call(bwd_kernel,grid=(pairs,),
        in_specs=[col,col,col,rows,rows,pl.BlockSpec((2,length,length),lambda g:(g,0,0)),col],
        out_specs=[col,col,col,rowst,rowst],
        out_shape=[cs,cs,cs,jax.ShapeDtypeStruct((width,2*length),f32),jax.ShapeDtypeStruct((width,2*length),f32)],
        scratch_shapes=[pltpu.VMEM((2,length,length),jnp.bfloat16),pltpu.VMEM((length,2*HEAD),jnp.bfloat16),pltpu.VMEM((2*HEAD,length),f32),pltpu.VMEM((2*HEAD,2*length),f32),pltpu.VMEM((2*HEAD,2*length),f32)],
        compiler_params=pltpu.CompilerParams(vmem_limit_bytes=60*2**20))(q,k,v,kr,qr,p,dc)


def on_device(
    hidden_in,
    key_mask,
    bucket_of_offset,
    position_table,
    query_weight,
    query_bias,
    key_weight,
    key_bias,
    value_weight,
    value_bias,
    out_weight,
    out_bias,
    first_gain,
    first_shift,
    up_weight,
    up_bias,
    down_weight,
    down_bias,
    second_gain,
    second_shift,
    cotangent,
):
    tokens = hidden_in.shape[0]
    length = LEN
    width_loc = query_weight.shape[1]
    mp_parts = lax.axis_size("mp")
    share_rows = tokens // mp_parts
    my_index = lax.axis_index("mp")

    def project(weight, bias_vec):
        return (
            jnp.dot(hidden_in, weight, preferred_element_type=jnp.float32)
            + bias_vec.astype(jnp.float32)
        ).astype(jnp.bfloat16)

    queries = project(query_weight, query_bias)
    keys_all = project(key_weight, key_bias)
    values_all = project(value_weight, value_bias)
    pos_query = (
        jnp.dot(position_table, query_weight, preferred_element_type=jnp.float32)
        + query_bias.astype(jnp.float32)
    ).astype(jnp.bfloat16)
    pos_key = (
        jnp.dot(position_table, key_weight, preferred_element_type=jnp.float32)
        + key_bias.astype(jnp.float32)
    ).astype(jnp.bfloat16)
    table_rows = position_table.shape[0]
    row_ids = jnp.arange(table_rows, dtype=jnp.int32)[None, :]
    falling = jnp.concatenate([bucket_of_offset[:1], bucket_of_offset[::-1]])
    rising = jnp.concatenate([bucket_of_offset, bucket_of_offset[:1]])
    hot_falling = (falling[:, None] == row_ids).astype(jnp.bfloat16)
    hot_rising = (rising[:, None] == row_ids).astype(jnp.bfloat16)

    def expand(one_hot, rows):
        return jnp.dot(one_hot, rows, preferred_element_type=jnp.float32).astype(jnp.bfloat16)

    key_rows = expand(hot_falling, pos_key)
    query_rows = expand(hot_falling, pos_query)
    query_rows_up = expand(hot_rising, pos_query)
    probs, context = attn_fwd(
        queries, keys_all, values_all, key_rows, query_rows, key_mask.reshape(1, length)
    )
    attn_share = lax.psum_scatter(
        jnp.dot(
            take_rows(context, jnp.int32(0), share_rows * lax.axis_size("mp")),
            out_weight,
            preferred_element_type=jnp.float32,
        ).astype(jnp.bfloat16),
        "mp",
        scatter_dimension=0,
        tiled=True,
    ).astype(jnp.float32)
    own_rows = take_rows(hidden_in, my_index * share_rows, share_rows).astype(jnp.float32)
    pre_first = attn_share + out_bias.astype(jnp.float32) + own_rows
    normed, first_pull = jax.vjp(
        norm_rows, pre_first, first_gain.astype(jnp.float32), first_shift.astype(jnp.float32)
    )
    normed_low = normed.astype(jnp.bfloat16)
    gathered = lax.all_gather(normed_low, "mp", axis=0, tiled=True)
    inner_pre = jnp.dot(gathered, up_weight, preferred_element_type=jnp.float32) + up_bias.astype(
        jnp.float32
    )
    activated, gelu_pull = jax.vjp(exact_gelu, inner_pre)
    act_low = activated.astype(jnp.bfloat16)
    down_share = lax.psum_scatter(
        jnp.dot(
            take_rows(act_low, jnp.int32(0), share_rows * lax.axis_size("mp")),
            down_weight,
            preferred_element_type=jnp.float32,
        ).astype(jnp.bfloat16),
        "mp",
        scatter_dimension=0,
        tiled=True,
    ).astype(jnp.float32)
    pre_second = down_share + down_bias.astype(jnp.float32) + normed
    result, second_pull = jax.vjp(
        norm_rows, pre_second, second_gain.astype(jnp.float32), second_shift.astype(jnp.float32)
    )
    d_pre_second, second_gain_grad, second_shift_grad = second_pull(cotangent.astype(jnp.float32))
    down_bias_grad = jnp.sum(d_pre_second, axis=0)
    d_down = d_pre_second.astype(jnp.bfloat16)
    part_rows = lax.all_gather(d_down, "mp", axis=0, tiled=True)
    row_count = part_rows.shape[0]
    weight_acc = left_product(take_rows(act_low, jnp.int32(0), row_count), part_rows)
    act_grad = right_product(part_rows, down_weight)
    down_weight_grad, act_grad = (weight_acc, act_grad)
    d_inner = gelu_pull(act_grad)[0].astype(jnp.bfloat16)
    up_bias_grad = jnp.sum(d_inner.astype(jnp.float32), axis=0)
    up_weight_grad = left_product(gathered, d_inner)
    d_normed = (
        lax.psum_scatter(
            right_product(
                take_rows(d_inner, jnp.int32(0), share_rows * lax.axis_size("mp")), up_weight
            ).astype(jnp.bfloat16),
            "mp",
            scatter_dimension=0,
            tiled=True,
        ).astype(jnp.float32)
        + d_pre_second
    )
    d_pre_first, first_gain_grad, first_shift_grad = first_pull(d_normed)
    out_bias_grad = jnp.sum(d_pre_first, axis=0)
    d_attn = d_pre_first.astype(jnp.bfloat16)
    part_rows = lax.all_gather(d_attn, "mp", axis=0, tiled=True)
    row_count = part_rows.shape[0]
    weight_acc = left_product(take_rows(context, jnp.int32(0), row_count), part_rows)
    ctx_grad = right_product(part_rows, out_weight)
    out_weight_grad, ctx_grad = (weight_acc, ctx_grad)
    d_context = ctx_grad.astype(jnp.bfloat16)
    d_query, d_key, d_value, key_rows_grad, query_rows_grad = attn_bwd(
        queries, keys_all, values_all, key_rows, query_rows_up, probs, d_context
    )
    d_pos_query = jnp.dot(
        query_rows_grad.astype(jnp.bfloat16), hot_rising, preferred_element_type=jnp.float32
    ).T
    d_pos_key = jnp.dot(
        key_rows_grad.astype(jnp.bfloat16), hot_falling, preferred_element_type=jnp.float32
    ).T
    query_weight_grad = left_product(hidden_in, d_query) + left_wide(position_table, d_pos_query)
    key_weight_grad = left_product(hidden_in, d_key) + left_wide(position_table, d_pos_key)
    value_weight_grad = left_product(hidden_in, d_value)
    query_bias_grad = jnp.sum(d_query.astype(jnp.float32), axis=0) + jnp.sum(query_rows_grad, axis=1)
    key_bias_grad = jnp.sum(d_key.astype(jnp.float32), axis=0) + jnp.sum(key_rows_grad, axis=1)
    value_bias_grad = jnp.sum(d_value.astype(jnp.float32), axis=0)
    table_grad = right_wide(d_pos_query, query_weight) + right_wide(d_pos_key, key_weight)
    start_at = jnp.int32(0)
    input_grad = (
        lax.psum_scatter(
            (
                right_product(
                    take_rows(d_query, start_at, lax.axis_size("mp") * share_rows), query_weight
                )
                + right_product(
                    take_rows(d_key, start_at, lax.axis_size("mp") * share_rows), key_weight
                )
                + right_product(
                    take_rows(d_value, start_at, lax.axis_size("mp") * share_rows), value_weight
                )
            ).astype(jnp.bfloat16),
            "mp",
            scatter_dimension=0,
            tiled=True,
        ).astype(jnp.float32)
        + d_pre_first
    )
    (
        query_weight_grad,
        query_bias_grad,
        key_weight_grad,
        key_bias_grad,
        value_weight_grad,
        value_bias_grad,
        out_weight_grad,
        up_weight_grad,
        up_bias_grad,
        down_weight_grad,
    ) = (
        lax.psum(query_weight_grad.astype(jnp.bfloat16), "dp").astype(jnp.float32),
        lax.psum(query_bias_grad.astype(jnp.bfloat16), "dp").astype(jnp.float32),
        lax.psum(key_weight_grad.astype(jnp.bfloat16), "dp").astype(jnp.float32),
        lax.psum(key_bias_grad.astype(jnp.bfloat16), "dp").astype(jnp.float32),
        lax.psum(value_weight_grad.astype(jnp.bfloat16), "dp").astype(jnp.float32),
        lax.psum(value_bias_grad.astype(jnp.bfloat16), "dp").astype(jnp.float32),
        lax.psum(out_weight_grad.astype(jnp.bfloat16), "dp").astype(jnp.float32),
        lax.psum(up_weight_grad.astype(jnp.bfloat16), "dp").astype(jnp.float32),
        lax.psum(up_bias_grad.astype(jnp.bfloat16), "dp").astype(jnp.float32),
        lax.psum(down_weight_grad.astype(jnp.bfloat16), "dp").astype(jnp.float32),
    )
    (
        table_grad,
        out_bias_grad,
        first_gain_grad,
        first_shift_grad,
        down_bias_grad,
        second_gain_grad,
        second_shift_grad,
    ) = lax.psum(
        (
            table_grad,
            out_bias_grad,
            first_gain_grad,
            first_shift_grad,
            down_bias_grad,
            second_gain_grad,
            second_shift_grad,
        ),
        ("dp", "mp"),
    )
    return (
        result.astype(jnp.bfloat16),
        input_grad,
        table_grad,
        query_weight_grad,
        query_bias_grad,
        key_weight_grad,
        key_bias_grad,
        value_weight_grad,
        value_bias_grad,
        out_weight_grad,
        out_bias_grad,
        first_gain_grad,
        first_shift_grad,
        up_weight_grad,
        up_bias_grad,
        down_weight_grad,
        down_bias_grad,
        second_gain_grad,
        second_shift_grad,
    )


def solution(mesh):
    return jax.shard_map(
        on_device,
        mesh=mesh,
        in_specs=(
            P("dp", None),
            P("dp"),
            P(),
            P(),
            P(None, "mp"),
            P("mp"),
            P(None, "mp"),
            P("mp"),
            P(None, "mp"),
            P("mp"),
            P("mp", None),
            P(),
            P(),
            P(),
            P(None, "mp"),
            P("mp"),
            P("mp", None),
            P(),
            P(),
            P(),
            P(("dp", "mp"), None),
        ),
        out_specs=(
            P(("dp", "mp"), None),
            P(("dp", "mp"), None),
            P(),
            P(None, "mp"),
            P("mp"),
            P(None, "mp"),
            P("mp"),
            P(None, "mp"),
            P("mp"),
            P("mp", None),
            P(),
            P(),
            P(),
            P(None, "mp"),
            P("mp"),
            P("mp", None),
            P(),
            P(),
            P(),
        ),
        check_vma=False,
    )
```

```python
import functools
import math

import jax
import jax.numpy as jnp
from jax import lax
from jax.experimental import pallas as pl
from jax.experimental.pallas import tpu as pltpu
from jax.sharding import PartitionSpec as P

HEAD = 64
PAIR = 2 * HEAD
LEN = 1024
BLK = 128

NORM_EPS = 1e-07
MASK_FILL = -1000000000.0
SCALE = 1.0 / math.sqrt(3.0 * HEAD)

F32 = jnp.float32
BF16 = jnp.bfloat16

NN = (((1,), (0,)), ((), ()))
NT = (((1,), (1,)), ((), ()))
TN = (((0,), (0,)), ((), ()))


def dot(left, right, dims=NN):
    return lax.dot_general(left, right, dims, preferred_element_type=F32)


def ordered(kernel, inputs, deps):
    def body(*refs):
        kernel(*refs[:inputs], *refs[inputs + len(deps) :])

    return body


def half_of(values, half):
    lane = lax.broadcasted_iota(jnp.int32, (1, PAIR), 1)
    return jnp.where((lane >= HEAD) if half else (lane < HEAD), values, jnp.zeros_like(values))


def join_halves(first, second):
    lane = lax.broadcasted_iota(jnp.int32, (1, PAIR), 1)
    return jnp.where(lane < HEAD, first, second)


def unit_matrix(flipped):
    row = lax.broadcasted_iota(jnp.int32, (BLK, BLK), 0)
    col = lax.broadcasted_iota(jnp.int32, (BLK, BLK), 1)
    hit = (row + col == BLK - 1) if flipped else (row == col)
    return hit.astype(F32).astype(BF16)


def shear(values):
    return pltpu.roll(values, 0, 1, stride=1, stride_axis=0)[:, BLK:]


def spread(values, base):
    wide = jnp.concatenate([values, jnp.zeros((values.shape[0], BLK), values.dtype)], axis=1)
    return pltpu.roll(wide, base, 1, stride=1, stride_axis=0)


def fwd_kernel(q_ref, k_ref, v_ref, kr_ref, qr_ref, mask_ref, p_ref, ctx_ref, from_scr):
    length = k_ref.shape[0]
    span = length + BLK
    step = pl.program_id(0)

    @pl.when(step == 0)
    def _():
        def from_rows(b, carry):
            j0 = pl.multiple_of(b * BLK, BLK)
            slab = qr_ref[pl.ds(pl.multiple_of(length - BLK - j0, BLK), span), :]
            kb = k_ref[pl.ds(j0, BLK), :]
            for half in (0, 1):
                part = dot(half_of(kb, half), slab, NT)
                from_scr[half, pl.ds(j0, BLK), :] = shear(part).astype(BF16)
            return carry

        lax.fori_loop(0, length // BLK, from_rows, 0)

    ident = unit_matrix(False)
    live = mask_ref[...] > 0
    i0 = pl.multiple_of(step * BLK, BLK)
    slab = kr_ref[pl.ds(pl.multiple_of(length - BLK - i0, BLK), span), :]
    qb = q_ref[pl.ds(i0, BLK), :]
    parts = []
    for half in (0, 1):
        qm = half_of(qb, half)
        to_pos = shear(dot(qm, slab, NT))
        left = jnp.concatenate([ident, qm], axis=1)
        right = jnp.concatenate([from_scr[half, :, pl.ds(i0, BLK)], k_ref[...]], axis=1)
        score = (dot(left, right, NT) + to_pos) * SCALE
        score = jnp.where(live, score, MASK_FILL)
        expd = jnp.exp(score - jnp.max(score, axis=1, keepdims=True))
        prob = (expd * (1.0 / jnp.sum(expd, axis=1, keepdims=True))).astype(BF16)
        p_ref[half] = prob
        parts.append(dot(prob, v_ref[...]))
    ctx_ref[...] = join_halves(parts[0], parts[1]).astype(BF16)


def attn_fwd(pair, q, k, v, kr, qr, mask, deps=()):
    length = q.shape[0]
    col = pl.BlockSpec((length, PAIR), lambda i: (0, pair))
    rows = pl.BlockSpec((2 * length, PAIR), lambda i: (0, pair))
    return pl.pallas_call(
        ordered(fwd_kernel, 6, deps),
        grid=(length // BLK,),
        in_specs=[col, col, col, rows, rows, pl.BlockSpec((1, length), lambda i: (0, 0))]
        + [pl.BlockSpec(memory_space=pl.ANY)] * len(deps),
        out_specs=[
            pl.BlockSpec((2, BLK, length), lambda i: (0, i, 0)),
            pl.BlockSpec((BLK, PAIR), lambda i: (i, 0)),
        ],
        out_shape=[
            pltpu.HBM((2, length, length), BF16),
            jax.ShapeDtypeStruct((length, PAIR), BF16),
        ],
        scratch_shapes=[pltpu.VMEM((2, length, length), BF16)],
        compiler_params=pltpu.CompilerParams(vmem_limit_bytes=40 * 2**20),
        cost_estimate=pl.CostEstimate(
            flops=128 * length * length * PAIR, bytes_accessed=10 * 2**20, transcendentals=2 * length * length
        ),
        name="attn_fwd",
    )(q, k, v, kr, qr, mask, *deps)


def bwd_rows_kernel(
    q_ref, k_ref, v_ref, kr_ref, p_ref, dc_ref, dq_ref, dv_ref, dkr_ref, ds_ref, qrev_ref, dv_scr, dkr_scr
):
    length = k_ref.shape[0]
    span = length + BLK
    step = pl.program_id(0)
    last = pl.num_programs(0) - 1

    @pl.when(step == 0)
    def _():
        dv_scr[...] = jnp.zeros_like(dv_scr)
        dkr_scr[...] = jnp.zeros_like(dkr_scr)

    rev = unit_matrix(True)
    i0 = pl.multiple_of(step * BLK, BLK)
    u0 = pl.multiple_of(length - BLK - i0, BLK)
    slab = kr_ref[pl.ds(u0, span), :]
    qb = dot(rev, q_ref[pl.ds(i0, BLK), :]).astype(BF16)
    qrev_ref[...] = qb
    dcb = dc_ref[pl.ds(i0, BLK), :]
    dcr = dot(rev, dcb).astype(BF16)
    parts = []
    dv_part = 0.0
    dkr_part = 0.0
    for half in (0, 1):
        prob = p_ref[half]
        d_prob = dot(half_of(dcr, half), v_ref[...], NT)
        prob_rev = dot(rev, prob)
        weighted = prob_rev * d_prob
        d_score = weighted - prob_rev * jnp.sum(weighted, axis=1, keepdims=True)
        d_low = d_score.astype(BF16)
        ds_ref[half] = d_low
        d_to = spread(d_score, 1).astype(BF16)
        parts.append(dot(d_low, k_ref[...]) + dot(d_to, slab))
        dv_part = dv_part + dot(half_of(dcb, half), prob, TN)
        dkr_part = dkr_part + dot(half_of(qb, half), d_to, TN)
    dqb = (join_halves(parts[0], parts[1]) * SCALE).astype(BF16)
    dq_ref[...] = dot(rev, dqb).astype(BF16)
    dv_scr[...] += dv_part
    dkr_scr[:, pl.ds(u0, span)] += dkr_part

    @pl.when(step == last)
    def _():
        dv_ref[...] = dv_scr[...].T.astype(BF16)
        dkr_ref[...] = (dkr_scr[...] * SCALE).astype(BF16)


def attn_bwd_rows(pair, q, k, v, kr, p, dc, deps=()):
    length = q.shape[0]
    steps = length // BLK
    col = pl.BlockSpec((length, PAIR), lambda i: (0, pair))
    whole = pl.BlockSpec((length, PAIR), lambda i: (0, 0))
    turned = pl.BlockSpec((BLK, PAIR), lambda i: (steps - 1 - i, 0))
    cols = jax.ShapeDtypeStruct((length, PAIR), BF16)
    return pl.pallas_call(
        ordered(bwd_rows_kernel, 6, deps),
        grid=(steps,),
        in_specs=[
            col,
            col,
            col,
            pl.BlockSpec((2 * length, PAIR), lambda i: (0, pair)),
            pl.BlockSpec((2, BLK, length), lambda i: (0, i, 0)),
            col,
        ]
        + [pl.BlockSpec(memory_space=pl.ANY)] * len(deps),
        out_specs=[
            pl.BlockSpec((BLK, PAIR), lambda i: (i, 0)),
            whole,
            pl.BlockSpec((PAIR, 2 * length), lambda i: (0, 0)),
            pl.BlockSpec((2, BLK, length), lambda i: (0, steps - 1 - i, 0)),
            turned,
        ],
        out_shape=[
            cols,
            cols,
            jax.ShapeDtypeStruct((PAIR, 2 * length), BF16),
            pltpu.HBM((2, length, length), BF16),
            cols,
        ],
        scratch_shapes=[pltpu.VMEM((PAIR, length), F32), pltpu.VMEM((PAIR, 2 * length), F32)],
        compiler_params=pltpu.CompilerParams(vmem_limit_bytes=40 * 2**20),
        cost_estimate=pl.CostEstimate(
            flops=128 * length * length * PAIR, bytes_accessed=10 * 2**20, transcendentals=0
        ),
        name="attn_bwd_rows",
    )(q, k, v, kr, p, dc, *deps)


def bwd_cols_kernel(k_ref, qr_ref, ds_ref, qrev_ref, dk_ref, dqr_ref, dqr_scr):
    length = k_ref.shape[0]
    span = length + BLK
    step = pl.program_id(0)
    last = pl.num_programs(0) - 1

    @pl.when(step == 0)
    def _():
        dqr_scr[...] = jnp.zeros_like(dqr_scr)

    ident = unit_matrix(False)
    j0 = pl.multiple_of(step * BLK, BLK)
    slab = qr_ref[pl.ds(j0, span), :]
    kb = k_ref[pl.ds(j0, BLK), :]
    parts = []
    dqr_part = 0.0
    for half in (0, 1):
        turned = dot(ident, ds_ref[half], NT)
        d_from = spread(turned, 0).astype(BF16)
        parts.append(dot(turned.astype(BF16), qrev_ref[...]) + dot(d_from, slab))
        dqr_part = dqr_part + dot(half_of(kb, half), d_from, TN)
    dk_ref[...] = (join_halves(parts[0], parts[1]) * SCALE).astype(BF16)
    dqr_scr[:, pl.ds(j0, span)] += dqr_part

    @pl.when(step == last)
    def _():
        dqr_ref[...] = (dqr_scr[...] * SCALE).astype(BF16)


def attn_bwd_cols(pair, k, qr, ds, qrev, deps=()):
    length = k.shape[0]
    return pl.pallas_call(
        ordered(bwd_cols_kernel, 4, deps),
        grid=(length // BLK,),
        in_specs=[
            pl.BlockSpec((length, PAIR), lambda i: (0, pair)),
            pl.BlockSpec((2 * length, PAIR), lambda i: (0, pair)),
            pl.BlockSpec((2, length, BLK), lambda i: (0, 0, i)),
            pl.BlockSpec((length, PAIR), lambda i: (0, 0)),
        ]
        + [pl.BlockSpec(memory_space=pl.ANY)] * len(deps),
        out_specs=[
            pl.BlockSpec((BLK, PAIR), lambda i: (i, 0)),
            pl.BlockSpec((PAIR, 2 * length), lambda i: (0, 0)),
        ],
        out_shape=[
            jax.ShapeDtypeStruct((length, PAIR), BF16),
            jax.ShapeDtypeStruct((PAIR, 2 * length), BF16),
        ],
        scratch_shapes=[pltpu.VMEM((PAIR, 2 * length), F32)],
        compiler_params=pltpu.CompilerParams(vmem_limit_bytes=40 * 2**20),
        cost_estimate=pl.CostEstimate(
            flops=88 * length * length * PAIR, bytes_accessed=10 * 2**20, transcendentals=0
        ),
        name="attn_bwd_cols",
    )(k, qr, ds, qrev, *deps)


def to_16(rows):
    more = -rows.shape[0] % 16
    if more:
        rows = jnp.concatenate([rows, jnp.zeros((more, rows.shape[1]), rows.dtype)], axis=0)
    return rows


def up_16(count):
    return count + -count % 16


def pack_kernel(parts, at_ref, *refs):
    d_refs, g_refs = refs[:6], refs[6:10]
    hidden_ref, table_ref, rising_ref, falling_ref, vec_ref, out_ref = refs[10:]
    table_rows = table_ref.shape[0]
    length = rising_ref.shape[1]
    bucket = lax.broadcasted_iota(jnp.int32, (table_rows, length), 0)
    weights = []
    positions = []
    biases = []
    for which in range(3):
        d_both = jnp.concatenate([d_refs[2 * which][...], d_refs[2 * which + 1][...]], axis=1)
        grad = dot(d_both, hidden_ref[...], TN)
        bias = jnp.sum(d_both.astype(F32), axis=0, keepdims=True)
        if which < 2:
            index_ref = (rising_ref, falling_ref)[which]
            hot = (bucket == index_ref[...]).astype(F32).astype(BF16)
            rows = jnp.concatenate([g_refs[2 * which][...], g_refs[2 * which + 1][...]], axis=0)
            pos = dot(hot, rows, NT)
            bias = bias + jnp.sum(pos, axis=0, keepdims=True)
            grad = grad + dot(pos.astype(BF16), table_ref[...], TN)
            positions.append(pos)
        weights.append(grad)
        biases.append(bias)
    weights = jnp.concatenate(weights, axis=0)
    positions = jnp.concatenate(positions, axis=1)
    width = weights.shape[1]
    biases = jnp.concatenate(biases, axis=1)
    biases = jnp.concatenate([biases, jnp.zeros((1, width - biases.shape[1]), F32)], axis=1)
    mine = lax.broadcasted_iota(jnp.int32, (16, width), 0) == at_ref[0]
    vectors = vec_ref[...] + jnp.where(mine, biases, 0.0)
    step = weights.shape[0] // parts
    half = table_rows // parts // 2
    for b in range(parts):
        pos = positions[2 * b * half : 2 * (b + 1) * half]
        out_ref[b] = jnp.concatenate(
            [
                to_16(weights[b * step : (b + 1) * step]),
                to_16(jnp.concatenate([pos[:half], pos[half:]], axis=1)),
                vectors if b == 0 else jnp.zeros_like(vectors),
            ],
            axis=0,
        ).astype(BF16)


def pack(parts, at, d_parts, grads, hidden, table, rising, falling, vectors, deps=()):
    width = hidden.shape[1]
    cols = 6 * PAIR
    rows = up_16(cols // parts) + up_16(table.shape[0] // parts // 2) + 16
    return pl.pallas_call(
        ordered(functools.partial(pack_kernel, parts), 16, deps),
        in_specs=[pl.BlockSpec(memory_space=pltpu.SMEM)]
        + [pl.BlockSpec(memory_space=pltpu.VMEM)] * 15
        + [pl.BlockSpec(memory_space=pl.ANY)] * len(deps),
        out_specs=pl.BlockSpec(memory_space=pltpu.VMEM),
        out_shape=jax.ShapeDtypeStruct((parts, rows, width), BF16),
        compiler_params=pltpu.CompilerParams(vmem_limit_bytes=48 * 2**20),
        cost_estimate=pl.CostEstimate(flops=8 * 10**9, bytes_accessed=10 * 2**20, transcendentals=0),
        name="pack",
    )(at, *d_parts, *grads, hidden, table, rising, falling, vectors, *deps)


def unpack_kernel(step, table_step, in_ref, q_ref, k_ref, v_ref, table_ref, vec_ref):
    parts = in_ref.shape[0]
    rows = up_16(step)
    weights = jnp.concatenate([in_ref[b, :rows].astype(F32)[:step] for b in range(parts)], axis=0)
    width = q_ref.shape[1]
    for i, ref in enumerate((q_ref, k_ref, v_ref)):
        ref[...] = weights[i * width : (i + 1) * width].T
    table = [in_ref[b, rows : rows + up_16(table_step)].astype(F32)[:table_step] for b in range(parts)]
    table_ref[...] = jnp.concatenate(table, axis=0)
    vec_ref[...] = in_ref[0, rows + up_16(table_step) :].astype(F32)


def unpack(whole, cols, table_rows):
    parts, _, width = whole.shape
    weight = jax.ShapeDtypeStruct((width, cols), F32)
    return pl.pallas_call(
        functools.partial(unpack_kernel, 3 * cols // parts, table_rows // parts),
        in_specs=[pl.BlockSpec(memory_space=pltpu.VMEM)],
        out_specs=[pl.BlockSpec(memory_space=pltpu.VMEM)] * 5,
        out_shape=[weight] * 3
        + [jax.ShapeDtypeStruct((table_rows, width), F32), jax.ShapeDtypeStruct((16, width), F32)],
        compiler_params=pltpu.CompilerParams(vmem_limit_bytes=48 * 2**20),
        name="unpack",
    )(whole)


def widen_kernel(in_ref, *refs):
    rows = in_ref[0].astype(F32)
    start = 0
    for ref in refs:
        ref[...] = rows[start : start + ref.shape[0]]
        start += ref.shape[0]


def widen(gathered, counts):
    parts, rows, width = gathered.shape
    return pl.pallas_call(
        widen_kernel,
        grid=(parts,),
        in_specs=[pl.BlockSpec((1, rows, width), lambda b: (b, 0, 0))],
        out_specs=[pl.BlockSpec((count, width), lambda b: (b, 0)) for count in counts],
        out_shape=[jax.ShapeDtypeStruct((parts * count, width), F32) for count in counts],
        cost_estimate=pl.CostEstimate(flops=0, bytes_accessed=6 * parts * rows * width, transcendentals=0),
        name="widen",
    )(gathered)


def swap(values, axis, mask):
    return lax.ppermute(values, axis, [(i, i ^ mask) for i in range(lax.axis_size(axis))])


def after(value, *deps):
    return lax.optimization_barrier((value, *deps))[0]


def pick(values, index, axis=0):
    return lax.dynamic_index_in_dim(values, index, axis, keepdims=False)


def bit_of(axis, mask):
    return (lax.axis_index(axis) & mask) // mask


def add_low(left, right):
    return (left.astype(F32) + right.astype(F32)).astype(BF16)


def pick_bit(values, at, low, bit):
    shape = values.shape
    cut = values.reshape(shape[:at] + (shape[at] // (2 * low), 2, low) + shape[at + 1 :])
    part = pick(cut, bit, at + 1)
    return part.reshape(shape[:at] + (shape[at] // 2,) + shape[at + 1 :])


def send_together(arrays, axis, mask):
    last = arrays[0].shape[-1]
    got = swap(jnp.concatenate([a.reshape(-1, last) for a in arrays], axis=0), axis, mask)
    parts = []
    start = 0
    for a in arrays:
        rows = a.size // last
        parts.append(got[start : start + rows].reshape(a.shape))
        start += rows
    return parts


def halve(arrays, ats, low, mask):
    bit = bit_of("dp", mask)
    theirs = send_together([pick_bit(a, at, low, 1 - bit) for a, at in zip(arrays, ats)], "dp", mask)
    return [pick_bit(a, at, low, bit) for a, at in zip(arrays, ats)], theirs


def add_all(pair):
    return [add_low(mine, theirs) for mine, theirs in zip(*pair)]


def low_sum_over(values, axis):
    mask = 1
    while mask < lax.axis_size(axis):
        values = add_low(values, swap(values, axis, mask))
        mask *= 2
    return values


def norm_parts(values):
    row_mean = jnp.mean(values, axis=-1, keepdims=True)
    centered = values - row_mean
    row_var = jnp.mean(centered * centered, axis=-1, keepdims=True)
    inverse = lax.rsqrt(row_var + NORM_EPS)
    return centered * inverse, inverse


def norm_back(grad, unit_rows, inverse, gain):
    d_unit = grad * gain
    mean_d = jnp.mean(d_unit, axis=-1, keepdims=True)
    mean_du = jnp.mean(d_unit * unit_rows, axis=-1, keepdims=True)
    return inverse * (d_unit - mean_d - unit_rows * mean_du)


def gelu_parts(values):
    cumulative = 0.5 + 0.5 * lax.erf(values * math.sqrt(0.5))
    density = jnp.exp(-0.5 * values * values) * (1.0 / math.sqrt(2.0 * math.pi))
    return values * cumulative, cumulative + values * density


def on_device(
    hidden_in,
    key_mask,
    bucket_of_offset,
    position_table,
    query_weight,
    query_bias,
    key_weight,
    key_bias,
    value_weight,
    value_bias,
    out_weight,
    out_bias,
    first_gain,
    first_shift,
    up_weight,
    up_bias,
    down_weight,
    down_bias,
    second_gain,
    second_shift,
    cotangent,
):
    tokens, width = hidden_in.shape
    width_loc = query_weight.shape[1]
    units = up_weight.shape[1]
    pairs = width_loc // PAIR
    dp_parts = lax.axis_size("dp")
    mp_parts = lax.axis_size("mp")
    dp_index = lax.axis_index("dp")
    mp_index = lax.axis_index("mp")
    share = tokens // mp_parts
    assert tokens == LEN and mp_parts == 4 and dp_parts & (dp_parts - 1) == 0
    dp_masks = [1 << b for b in range(dp_parts.bit_length() - 1)]
    others = range(1, mp_parts)

    def relative(blocks):
        return jnp.concatenate([pick(blocks, mp_index ^ s)[None] for s in range(mp_parts)], axis=0)

    def to_owners(blocks):
        return [blocks[0]] + [swap(blocks[s], "mp", s) for s in others]

    def by_owner(rows):
        blocks = rows.reshape(mp_parts, -1, rows.shape[1])
        return [pick(blocks, mp_index ^ s) for s in range(mp_parts)]

    def my_part(rows):
        count = rows.shape[0] // dp_parts
        return lax.dynamic_slice_in_dim(rows, dp_index * count, count, 0)

    out_slice = jnp.stack(to_owners([my_part(out_weight)] * mp_parts))
    out_all = jnp.swapaxes(lax.all_gather(out_slice, "dp", axis=0), 0, 1).reshape(width, width)
    bias_row = jnp.pad(up_bias.reshape(1, units), ((0, 15), (0, 0)))
    far_slice = jnp.concatenate([my_part(up_weight), my_part(down_weight), bias_row], axis=0)
    far_slice = swap(far_slice, "mp", 2)
    far_bias = far_slice[-16]

    def project(rows, weight, bias_vec):
        return (dot(rows, weight) + bias_vec.astype(F32)).astype(BF16)

    queries = project(hidden_in, query_weight, query_bias)
    keys_all = project(hidden_in, key_weight, key_bias)
    values_all = project(hidden_in, value_weight, value_bias)
    pos_query = project(position_table, query_weight, query_bias)
    pos_key = project(position_table, key_weight, key_bias)
    row_ids = jnp.arange(position_table.shape[0], dtype=jnp.int32)[None, :]
    falling = jnp.concatenate([bucket_of_offset[:1], bucket_of_offset[::-1]])
    rising = jnp.concatenate([bucket_of_offset, bucket_of_offset[:1]])
    hot_falling = (falling[:, None] == row_ids).astype(BF16)
    hot_rising = (rising[:, None] == row_ids).astype(BF16)
    key_rows = dot(hot_falling, pos_key).astype(BF16)
    query_rows = dot(hot_falling, pos_query).astype(BF16)
    query_rows_up = dot(hot_rising, pos_query).astype(BF16)

    weight_cat = jnp.concatenate([query_weight, key_weight, value_weight], axis=1)

    probs = []
    context = []
    for pair in range(pairs):
        prob, ctx = attn_fwd(
            pair, queries, keys_all, values_all, key_rows, query_rows, key_mask.reshape(1, tokens)
        )
        probs.append(prob)
        context.append(ctx)
        if pair == 0:
            far_all = lax.all_gather(after(far_slice, ctx), "dp", axis=0)
    context = jnp.concatenate(context, axis=1)
    ctx_rows = jnp.concatenate(to_owners(by_owner(context)), axis=1)

    own_rows = lax.dynamic_slice_in_dim(hidden_in, mp_index * share, share, 0)
    pre_first = dot(ctx_rows, out_all) + out_bias.astype(F32) + own_rows.astype(F32)
    unit_first, inverse_first = norm_parts(pre_first)
    gain_first = first_gain.astype(F32)
    normed = unit_first * gain_first + first_shift.astype(F32)
    normed_low = normed.astype(BF16)

    near_low = swap(normed_low, "mp", 1)
    up_cat = jnp.concatenate([up_weight, far_all[:, : width // dp_parts].reshape(width, units)], axis=1)
    down_cat = jnp.concatenate([down_weight, far_all[:, width // dp_parts : -16].reshape(units, width)], axis=0)
    bias_cat = jnp.concatenate([up_bias, far_bias], axis=0).astype(F32)

    def feed(rows):
        act, slope = gelu_parts(dot(rows, up_cat) + bias_cat)
        act_low = act.astype(BF16)
        return act_low, slope.astype(BF16), dot(act_low, down_cat)

    act_near, slope_near, mixed_near = feed(near_low)
    act_own, slope_own, mixed_own = feed(normed_low)
    mixed = mixed_own + swap(mixed_near.astype(BF16), "mp", 1).astype(F32)
    pre_second = mixed + down_bias.astype(F32) + normed

    unit_second, inverse_second = norm_parts(pre_second)
    gain_second = second_gain.astype(F32)
    layer_out = (unit_second * gain_second + second_shift.astype(F32)).astype(BF16)
    cot = cotangent.astype(F32)
    d_pre_second = norm_back(cot, unit_second, inverse_second, gain_second)
    d_down = d_pre_second.astype(BF16)

    near_d_down = swap(d_down, "mp", 1)

    def feed_back(d_rows, slope):
        d_inner = (dot(d_rows, down_cat, NT) * slope.astype(F32)).astype(BF16)
        return d_inner, dot(d_inner, up_cat, NT)

    d_inner_own, back_own = feed_back(d_down, slope_own)
    d_inner_near, back_near = feed_back(near_d_down, slope_near)
    back_near = swap(back_near.astype(BF16), "mp", 1)
    d_normed = back_own + back_near.astype(F32) + d_pre_second
    act_cat = jnp.concatenate([act_own, act_near], axis=0)
    d_down_cat = jnp.concatenate([d_down, near_d_down], axis=0)
    normed_cat = jnp.concatenate([normed_low, near_low], axis=0)
    d_inner_cat = jnp.concatenate([d_inner_own, d_inner_near], axis=0)

    half = dp_parts // 2

    def blocks_of(cols, which, groups):
        step = cols.shape[1] // (groups * dp_parts)
        return jnp.concatenate(
            [
                lax.dynamic_slice_in_dim(cols, (g * dp_parts + 2 * j + which) * step, step, 1)
                for g in range(groups)
                for j in range(half)
            ],
            axis=1,
        )

    def halves_sum(make):
        bit = bit_of("dp", 1)
        theirs = swap(make(1 - bit).astype(BF16), "dp", 1)
        return (make(bit) + theirs.astype(F32)).astype(BF16)

    down_sum = halves_sum(lambda which: dot(blocks_of(act_cat, which, 2), d_down_cat, TN))
    down_sum = down_sum.reshape(2, half, units // dp_parts, width)
    up_sum = halves_sum(lambda which: dot(blocks_of(normed_cat, which, 1), d_inner_cat, TN))
    up_sum = up_sum.reshape(half, width // dp_parts, 2 * units)
    up_bias_part = jnp.sum(d_inner_cat.astype(F32), axis=0)

    d_pre_first = norm_back(d_normed, unit_first, inverse_first, gain_first)
    d_attn = d_pre_first.astype(BF16)
    d_ctx = dot(d_attn, out_all, NT).astype(BF16)
    d_ctx_parts = jnp.stack(
        to_owners([d_ctx[:, s * width_loc : (s + 1) * width_loc] for s in range(mp_parts)])
    )
    out_sum = dot(ctx_rows, d_attn, TN).astype(BF16).reshape(mp_parts, dp_parts, -1, width)
    sums = jnp.stack(
        [
            jnp.sum(d_pre_first, axis=0),
            jnp.sum(d_normed * unit_first, axis=0),
            jnp.sum(d_normed, axis=0),
            jnp.sum(d_pre_second, axis=0),
            jnp.sum(cot * unit_second, axis=0),
            jnp.sum(cot, axis=0),
        ]
    )

    d_ctx = jnp.concatenate(
        [pick(d_ctx_parts, mp_index ^ s) for s in range(mp_parts)], axis=0
    )

    def rows_step(pair, deps):
        return attn_bwd_rows(pair, queries, keys_all, values_all, key_rows, probs[pair], d_ctx, deps)

    def cols_step(pair, deps):
        _, _, _, d_score, turned = by_rows[pair]
        return attn_bwd_cols(pair, keys_all, query_rows_up, d_score, turned, deps)

    low_bits = list(range(len(dp_masks) - 1))
    cut = max(1, len(low_bits) // 2)

    def steps(arrays, ats, bits, left):
        pair = None
        for bit in bits:
            pair = halve(arrays if pair is None else add_all(pair), ats, 1 << left.index(bit), 2 << bit)
            left.remove(bit)
        return pair

    def tied(pair, *deps):
        return pair[0], [after(theirs, *deps) for theirs in pair[1]]

    left_one, left_two = list(low_bits), list(low_bits)
    bits_one, bits_two = low_bits, low_bits[::-1]
    step_two = steps([up_sum], [0], bits_two[:cut], left_two)
    step_out = halve([out_sum], [1], 1, 1)
    step_one = steps([down_sum], [1], bits_one[:cut], left_one)
    by_rows = [rows_step(0, (up_sum, down_sum, step_out[0][0]))]
    (down_sum,) = add_all(tied(step_one, by_rows[0][1]))
    (up_sum,) = add_all(tied(step_two, by_rows[0][1]))
    (out_sum,) = add_all(tied(step_out, by_rows[0][1]))
    step_one = steps([down_sum], [1], bits_one[cut:], left_one)
    step_two = steps([up_sum], [0], bits_two[cut:], left_two)
    step_out = steps([out_sum], [1], bits_one[:cut], list(low_bits))
    by_rows.append(rows_step(1, (by_rows[0][1], down_sum, up_sum, out_sum)))
    d_query, d_value = (jnp.concatenate([r[i] for r in by_rows], axis=1) for i in (0, 1))
    key_grad = jnp.concatenate([r[2] for r in by_rows], axis=0)
    d_value1 = by_rows[1][1]
    (down_sum,) = add_all(tied(step_one, d_value1))
    (up_sum,) = add_all(tied(step_two, d_value1))
    (out_sum,) = add_all(tied(step_out, d_value1))
    step_out = steps([out_sum], [1], bits_one[cut:], low_bits[cut:])
    down_sum, up_sum = down_sum[:, 0], up_sum[0]
    down_rows = down_sum.shape[1]
    far = send_together([down_sum[1], up_sum[:, units:]], "mp", 2)
    by_cols = [cols_step(0, (down_sum, up_sum, out_sum))]
    (out_sum,) = add_all(tied(step_out, by_cols[0][0]))
    out_sum = out_sum[:, 0]
    out_rows = out_sum.shape[1]
    by_cols.append(cols_step(1, (by_cols[0][0], out_sum)))
    d_key = jnp.concatenate([r[0] for r in by_cols], axis=1)
    query_grad = jnp.concatenate([r[1] for r in by_cols], axis=0)
    out_parts = to_owners([out_sum[s] for s in range(mp_parts)])
    out_sum = out_parts[0].astype(F32) + sum(after(p, d_key).astype(F32) for p in out_parts[1:])
    far = [after(part, d_key) for part in far]
    ready = jnp.concatenate(
        [
            add_low(down_sum[0], far[0]),
            add_low(up_sum[:, :units], far[1]),
            out_sum.astype(BF16),
        ],
        axis=0,
    )
    gathered = lax.all_gather(ready, "dp", axis=0)
    d_key1 = after(by_cols[1][0], ready)
    down_weight_grad, up_weight_grad, out_weight_grad = widen(gathered, (down_rows, down_rows, out_rows))

    device_ids = jnp.arange(mp_parts)[:, None]
    up_bias_part = jnp.where(device_ids == mp_index, up_bias_part[:units], 0.0) + jnp.where(
        device_ids == (mp_index ^ 2), up_bias_part[units:], 0.0
    )
    vectors = jnp.concatenate([jnp.zeros_like(up_bias_part), sums, up_bias_part], axis=0)
    vectors = jnp.pad(vectors, ((0, 16 - vectors.shape[0]), (0, 0)))
    message = pack(
        dp_parts,
        mp_index.reshape(1),
        [by_rows[0][0], by_rows[1][0], by_cols[0][0], d_key1, by_rows[0][1], by_rows[1][1]],
        [by_cols[0][1], by_cols[1][1], by_rows[0][2], by_rows[1][2]],
        hidden_in,
        position_table,
        rising[None, :],
        falling[None, :],
        vectors,
    )

    (message,) = add_all(halve([message], [0], 1, 1))
    block_index = dp_index // 2
    total = pick(message, block_index).astype(F32)
    for s in range(1, half):
        total = total + swap(pick(message, block_index ^ s), "dp", 2 * s).astype(F32)
    step = 3 * width_loc // dp_parts
    table_rows = position_table.shape[0]
    table_step = table_rows // dp_parts
    packed = total[up_16(step) : up_16(step) + table_step // 2].astype(BF16)
    packed = jnp.concatenate([packed[:, : 2 * width_loc], packed[:, 2 * width_loc :]], axis=0)
    table_part = dot(packed, weight_cat[:, : 2 * width_loc], NT)
    shared_sum = jnp.concatenate([to_16(table_part), total[-16:]], axis=0).astype(BF16)
    shared_sum = low_sum_over(shared_sum, "mp")
    block = jnp.concatenate([total[: up_16(step)].astype(BF16), shared_sum], axis=0)
    d_cat = after(jnp.concatenate([d_query, d_key, d_value], axis=1), shared_sum, gathered)
    input_part = dot(d_cat, weight_cat, NT).astype(BF16)
    input_part = lax.psum_scatter(input_part, "mp", scatter_dimension=0, tiled=True)
    input_grad = d_pre_first + input_part.astype(F32)

    parts = jnp.stack([block] + [swap(block, "dp", 2 * s) for s in range(1, half)])
    mine = jnp.stack([pick(parts, block_index ^ j) for j in range(half)])
    mine = after(mine, down_weight_grad)
    theirs = swap(mine, "dp", 1)
    even = bit_of("dp", 1) == 0
    whole = jnp.stack([jnp.where(even, mine, theirs), jnp.where(even, theirs, mine)], axis=1)
    whole = whole.reshape(dp_parts, -1, width)
    query_weight_grad, key_weight_grad, value_weight_grad, table_grad, vectors = unpack(
        whole, width_loc, table_rows
    )
    biases = lax.dynamic_index_in_dim(vectors, mp_index, 0, keepdims=False)
    query_bias_grad, key_bias_grad, value_bias_grad = (
        biases[i * width_loc : (i + 1) * width_loc] for i in range(3)
    )
    shared_sums = vectors[mp_parts:]
    up_bias_grad = lax.dynamic_index_in_dim(vectors, mp_parts + 6 + mp_index, 0, keepdims=False)

    out_bias_grad, first_gain_grad, first_shift_grad, down_bias_grad, second_gain_grad, second_shift_grad = (
        shared_sums[i] for i in range(6)
    )
    return (
        layer_out,
        input_grad,
        table_grad,
        query_weight_grad,
        query_bias_grad,
        key_weight_grad,
        key_bias_grad,
        value_weight_grad,
        value_bias_grad,
        out_weight_grad,
        out_bias_grad,
        first_gain_grad,
        first_shift_grad,
        up_weight_grad,
        up_bias_grad,
        down_weight_grad,
        down_bias_grad,
        second_gain_grad,
        second_shift_grad,
    )


def solution(mesh):
    return jax.shard_map(
        on_device,
        mesh=mesh,
        in_specs=(
            P("dp", None),
            P("dp"),
            P(),
            P(),
            P(None, "mp"),
            P("mp"),
            P(None, "mp"),
            P("mp"),
            P(None, "mp"),
            P("mp"),
            P("mp", None),
            P(),
            P(),
            P(),
            P(None, "mp"),
            P("mp"),
            P("mp", None),
            P(),
            P(),
            P(),
            P(("dp", "mp"), None),
        ),
        out_specs=(
            P(("dp", "mp"), None),
            P(("dp", "mp"), None),
            P(),
            P(None, "mp"),
            P("mp"),
            P(None, "mp"),
            P("mp"),
            P(None, "mp"),
            P("mp"),
            P("mp", None),
            P(),
            P(),
            P(),
            P(None, "mp"),
            P("mp"),
            P("mp", None),
            P(),
            P(),
            P(),
        ),
        check_vma=False,
    )
```

```python
import functools
import math

import jax
import jax.numpy as jnp
from jax import lax
from jax.experimental import pallas as pl
from jax.experimental.pallas import tpu as pltpu
from jax.sharding import PartitionSpec as P

HEAD = 64
PAIR = 2 * HEAD
LEN = 1024
BLK = 256

NORM_EPS = 1e-07
MASK_FILL = -1000000000.0
SCALE = 1.0 / math.sqrt(3.0 * HEAD)

F32 = jnp.float32
BF16 = jnp.bfloat16

NN = (((1,), (0,)), ((), ()))
NT = (((1,), (1,)), ((), ()))
TN = (((0,), (0,)), ((), ()))


def dot(left, right, dims=NN):
    return lax.dot_general(left, right, dims, preferred_element_type=F32)


def ordered(kernel, inputs, deps):
    def body(*refs):
        kernel(*refs[:inputs], *refs[inputs + len(deps) :])

    return body


def half_of(values, half):
    lane = lax.broadcasted_iota(jnp.int32, (1, PAIR), 1)
    return jnp.where((lane >= HEAD) if half else (lane < HEAD), values, jnp.zeros_like(values))


def join_halves(first, second):
    lane = lax.broadcasted_iota(jnp.int32, (1, PAIR), 1)
    return jnp.where(lane < HEAD, first, second)


def unit_matrix(flipped):
    row = lax.broadcasted_iota(jnp.int32, (BLK, BLK), 0)
    col = lax.broadcasted_iota(jnp.int32, (BLK, BLK), 1)
    hit = (row + col == BLK - 1) if flipped else (row == col)
    return hit.astype(F32).astype(BF16)


def shear(values):
    return pltpu.roll(values, 0, 1, stride=1, stride_axis=0)[:, BLK:]


def spread(values, base):
    wide = jnp.concatenate([values, jnp.zeros((values.shape[0], BLK), values.dtype)], axis=1)
    return pltpu.roll(wide, base, 1, stride=1, stride_axis=0)


def project_kernel(hidden_ref, table_ref, rising_ref, falling_ref, *refs):
    weights, biases, outs = refs[:3], refs[3:6], refs[6:]
    table_rows = table_ref.shape[0]
    bucket = lax.broadcasted_iota(jnp.int32, (table_rows, rising_ref.shape[1]), 0)
    falling = (bucket == falling_ref[...]).astype(F32).astype(BF16)
    positions = []
    for i in range(3):
        bias = biases[i][...].astype(F32)
        if i < 2:
            positions.append((dot(table_ref[...], weights[i][...]) + bias).astype(BF16))
        outs[i][...] = (dot(hidden_ref[...], weights[i][...]) + bias).astype(BF16)
    outs[3][...] = dot(positions[1], falling, TN).astype(BF16)
    outs[4][...] = dot(positions[0], falling, TN).astype(BF16)
    rising = (bucket == rising_ref[...]).astype(F32).astype(BF16)
    outs[5][...] = dot(positions[0], rising, TN).astype(BF16)


def project(hidden, table, rising, falling, weights, biases):
    tokens = hidden.shape[0]
    width = weights[0].shape[1]
    operands = (hidden, table, rising, falling, *weights, *biases)
    outs = [jax.ShapeDtypeStruct((tokens, width), BF16)] * 3
    outs += [jax.ShapeDtypeStruct((width, rising.shape[1]), BF16)] * 3

    def full(array):
        return pl.BlockSpec(array.shape, lambda i: (0,) * len(array.shape))

    return pl.pallas_call(
        project_kernel,
        grid=(1,),
        in_specs=[full(array) for array in operands],
        out_specs=[full(array) for array in outs],
        out_shape=outs,
        compiler_params=pltpu.CompilerParams(vmem_limit_bytes=40 * 2**20),
        cost_estimate=pl.CostEstimate(flops=6 * 10**9, bytes_accessed=8 * 2**20, transcendentals=0),
        name="project",
    )(*operands)


def fwd_kernel(q_ref, k_ref, v_ref, kr_ref, qr_ref, mask_ref, p_ref, ctx_ref, from_scr):
    length = k_ref.shape[0]
    span = length + BLK
    step = pl.program_id(0)

    @pl.when(step == 0)
    def _():
        def from_rows(b, carry):
            j0 = pl.multiple_of(b * BLK, BLK)
            slab = qr_ref[:, pl.ds(pl.multiple_of(length - BLK - j0, BLK), span)]
            kb = k_ref[pl.ds(j0, BLK), :]
            for half in (0, 1):
                part = dot(half_of(kb, half), slab)
                from_scr[half, pl.ds(j0, BLK), :] = shear(part).astype(BF16)
            return carry

        lax.fori_loop(0, length // BLK, from_rows, 0)

    ident = unit_matrix(False)
    live = mask_ref[...] > 0
    i0 = pl.multiple_of(step * BLK, BLK)
    slab = kr_ref[:, pl.ds(pl.multiple_of(length - BLK - i0, BLK), span)]
    qb = q_ref[pl.ds(i0, BLK), :]
    parts = []
    for half in (0, 1):
        qm = half_of(qb, half)
        to_pos = shear(dot(qm, slab))
        left = jnp.concatenate([ident, qm], axis=1)
        right = jnp.concatenate([from_scr[half, :, pl.ds(i0, BLK)], k_ref[...]], axis=1)
        score = (dot(left, right, NT) + to_pos) * SCALE
        score = jnp.where(live, score, MASK_FILL)
        expd = jnp.exp(score - jnp.max(score, axis=1, keepdims=True))
        prob = (expd * (1.0 / jnp.sum(expd, axis=1, keepdims=True))).astype(BF16)
        p_ref[half] = prob
        parts.append(dot(prob, v_ref[...]))
    ctx_ref[...] = join_halves(parts[0], parts[1]).astype(BF16)


def attn_fwd(pair, q, k, v, kr, qr, mask, deps=()):
    length = q.shape[0]
    col = pl.BlockSpec((length, PAIR), lambda i: (0, pair))
    rows = pl.BlockSpec((PAIR, 2 * length), lambda i: (pair, 0))
    return pl.pallas_call(
        ordered(fwd_kernel, 6, deps),
        grid=(length // BLK,),
        in_specs=[col, col, col, rows, rows, pl.BlockSpec((1, length), lambda i: (0, 0))]
        + [pl.BlockSpec(memory_space=pl.ANY)] * len(deps),
        out_specs=[
            pl.BlockSpec((2, BLK, length), lambda i: (0, i, 0)),
            pl.BlockSpec((BLK, PAIR), lambda i: (i, 0)),
        ],
        out_shape=[
            pltpu.HBM((2, length, length), BF16),
            jax.ShapeDtypeStruct((length, PAIR), BF16),
        ],
        scratch_shapes=[pltpu.VMEM((2, length, length), BF16)],
        compiler_params=pltpu.CompilerParams(vmem_limit_bytes=20 * 2**20),
        cost_estimate=pl.CostEstimate(
            flops=128 * length * length * PAIR, bytes_accessed=10 * 2**20, transcendentals=2 * length * length
        ),
        name="attn_fwd",
    )(q, k, v, kr, qr, mask, *deps)


def bwd_rows_kernel(
    q_ref, k_ref, v_ref, kr_ref, p_ref, dc_ref, dq_ref, dv_ref, dkr_ref, ds_ref, qrev_ref, dv_scr, dkr_scr
):
    length = k_ref.shape[0]
    span = length + BLK
    step = pl.program_id(0)
    last = pl.num_programs(0) - 1

    @pl.when(step == 0)
    def _():
        dv_scr[...] = jnp.zeros_like(dv_scr)
        dkr_scr[...] = jnp.zeros_like(dkr_scr)

    rev = unit_matrix(True)
    i0 = pl.multiple_of(step * BLK, BLK)
    u0 = pl.multiple_of(length - BLK - i0, BLK)
    slab = kr_ref[:, pl.ds(u0, span)]
    qb = dot(rev, q_ref[pl.ds(i0, BLK), :]).astype(BF16)
    qrev_ref[...] = qb
    dcb = dc_ref[pl.ds(i0, BLK), :]
    dcr = dot(rev, dcb).astype(BF16)
    parts = []
    dv_part = 0.0
    dkr_part = 0.0
    for half in (0, 1):
        prob = p_ref[half]
        d_prob = dot(half_of(dcr, half), v_ref[...], NT)
        prob_rev = dot(rev, prob)
        weighted = prob_rev * d_prob
        d_score = weighted - prob_rev * jnp.sum(weighted, axis=1, keepdims=True)
        d_low = d_score.astype(BF16)
        ds_ref[half] = d_low
        d_to = spread(d_score, 1).astype(BF16)
        parts.append(dot(d_low, k_ref[...]) + dot(d_to, slab, NT))
        dv_part = dv_part + dot(half_of(dcb, half), prob, TN)
        dkr_part = dkr_part + dot(half_of(qb, half), d_to, TN)
    dqb = (join_halves(parts[0], parts[1]) * SCALE).astype(BF16)
    dq_ref[...] = dot(rev, dqb).astype(BF16)
    dv_scr[...] += dv_part
    dkr_scr[:, pl.ds(u0, span)] += dkr_part

    @pl.when(step == last)
    def _():
        dv_ref[...] = dv_scr[...].T.astype(BF16)
        dkr_ref[...] = (dkr_scr[...] * SCALE).astype(BF16)


def attn_bwd_rows(pair, q, k, v, kr, p, dc, deps=()):
    length = q.shape[0]
    steps = length // BLK
    col = pl.BlockSpec((length, PAIR), lambda i: (0, pair))
    whole = pl.BlockSpec((length, PAIR), lambda i: (0, 0))
    turned = pl.BlockSpec((BLK, PAIR), lambda i: (steps - 1 - i, 0))
    cols = jax.ShapeDtypeStruct((length, PAIR), BF16)
    return pl.pallas_call(
        ordered(bwd_rows_kernel, 6, deps),
        grid=(steps,),
        in_specs=[
            col,
            col,
            col,
            pl.BlockSpec((PAIR, 2 * length), lambda i: (pair, 0)),
            pl.BlockSpec((2, BLK, length), lambda i: (0, i, 0)),
            col,
        ]
        + [pl.BlockSpec(memory_space=pl.ANY)] * len(deps),
        out_specs=[
            pl.BlockSpec((BLK, PAIR), lambda i: (i, 0)),
            whole,
            pl.BlockSpec((PAIR, 2 * length), lambda i: (0, 0)),
            pl.BlockSpec((2, BLK, length), lambda i: (0, steps - 1 - i, 0)),
            turned,
        ],
        out_shape=[
            cols,
            cols,
            jax.ShapeDtypeStruct((PAIR, 2 * length), BF16),
            pltpu.HBM((2, length, length), BF16),
            cols,
        ],
        scratch_shapes=[pltpu.VMEM((PAIR, length), F32), pltpu.VMEM((PAIR, 2 * length), F32)],
        compiler_params=pltpu.CompilerParams(vmem_limit_bytes=20 * 2**20),
        cost_estimate=pl.CostEstimate(
            flops=128 * length * length * PAIR, bytes_accessed=10 * 2**20, transcendentals=0
        ),
        name="attn_bwd_rows",
    )(q, k, v, kr, p, dc, *deps)


def bwd_cols_kernel(k_ref, qr_ref, ds_ref, qrev_ref, dk_ref, dqr_ref, dqr_scr):
    length = k_ref.shape[0]
    span = length + BLK
    step = pl.program_id(0)
    last = pl.num_programs(0) - 1

    @pl.when(step == 0)
    def _():
        dqr_scr[...] = jnp.zeros_like(dqr_scr)

    ident = unit_matrix(False)
    j0 = pl.multiple_of(step * BLK, BLK)
    slab = qr_ref[:, pl.ds(j0, span)]
    kb = k_ref[pl.ds(j0, BLK), :]
    parts = []
    dqr_part = 0.0
    for half in (0, 1):
        turned = dot(ident, ds_ref[half], NT)
        d_from = spread(turned, 0).astype(BF16)
        parts.append(dot(turned.astype(BF16), qrev_ref[...]) + dot(d_from, slab, NT))
        dqr_part = dqr_part + dot(half_of(kb, half), d_from, TN)
    dk_ref[...] = (join_halves(parts[0], parts[1]) * SCALE).astype(BF16)
    dqr_scr[:, pl.ds(j0, span)] += dqr_part

    @pl.when(step == last)
    def _():
        dqr_ref[...] = (dqr_scr[...] * SCALE).astype(BF16)


def attn_bwd_cols(pair, k, qr, ds, qrev, deps=()):
    length = k.shape[0]
    return pl.pallas_call(
        ordered(bwd_cols_kernel, 4, deps),
        grid=(length // BLK,),
        in_specs=[
            pl.BlockSpec((length, PAIR), lambda i: (0, pair)),
            pl.BlockSpec((PAIR, 2 * length), lambda i: (pair, 0)),
            pl.BlockSpec((2, length, BLK), lambda i: (0, 0, i)),
            pl.BlockSpec((length, PAIR), lambda i: (0, 0)),
        ]
        + [pl.BlockSpec(memory_space=pl.ANY)] * len(deps),
        out_specs=[
            pl.BlockSpec((BLK, PAIR), lambda i: (i, 0)),
            pl.BlockSpec((PAIR, 2 * length), lambda i: (0, 0)),
        ],
        out_shape=[
            jax.ShapeDtypeStruct((length, PAIR), BF16),
            jax.ShapeDtypeStruct((PAIR, 2 * length), BF16),
        ],
        scratch_shapes=[pltpu.VMEM((PAIR, 2 * length), F32)],
        compiler_params=pltpu.CompilerParams(vmem_limit_bytes=20 * 2**20),
        cost_estimate=pl.CostEstimate(
            flops=88 * length * length * PAIR, bytes_accessed=10 * 2**20, transcendentals=0
        ),
        name="attn_bwd_cols",
    )(k, qr, ds, qrev, *deps)


def to_16(rows):
    more = -rows.shape[0] % 16
    if more:
        rows = jnp.concatenate([rows, jnp.zeros((more, rows.shape[1]), rows.dtype)], axis=0)
    return rows


def up_16(count):
    return count + -count % 16


def pack_kernel(parts, at_ref, *refs):
    d_refs, g_refs = refs[:6], refs[6:10]
    hidden_ref, table_ref, rising_ref, falling_ref, vec_ref, out_ref = refs[10:]
    table_rows = table_ref.shape[0]
    length = rising_ref.shape[1]
    bucket = lax.broadcasted_iota(jnp.int32, (table_rows, length), 0)
    weights = []
    positions = []
    biases = []
    for which in range(3):
        d_both = jnp.concatenate([d_refs[2 * which][...], d_refs[2 * which + 1][...]], axis=1)
        grad = dot(d_both, hidden_ref[...], TN)
        bias = jnp.sum(d_both.astype(F32), axis=0, keepdims=True)
        if which < 2:
            index_ref = (rising_ref, falling_ref)[which]
            hot = (bucket == index_ref[...]).astype(F32).astype(BF16)
            rows = jnp.concatenate([g_refs[2 * which][...], g_refs[2 * which + 1][...]], axis=0)
            pos = dot(hot, rows, NT)
            bias = bias + jnp.sum(pos, axis=0, keepdims=True)
            grad = grad + dot(pos.astype(BF16), table_ref[...], TN)
            positions.append(pos)
        weights.append(grad)
        biases.append(bias)
    weights = jnp.concatenate(weights, axis=0)
    positions = jnp.concatenate(positions, axis=1)
    width = weights.shape[1]
    biases = jnp.concatenate(biases, axis=1)
    biases = jnp.concatenate([biases, jnp.zeros((1, width - biases.shape[1]), F32)], axis=1)
    mine = lax.broadcasted_iota(jnp.int32, (16, width), 0) == at_ref[0]
    vectors = vec_ref[...] + jnp.where(mine, biases, 0.0)
    step = weights.shape[0] // parts
    half = table_rows // parts // 2
    for b in range(parts):
        pos = positions[2 * b * half : 2 * (b + 1) * half]
        out_ref[b] = jnp.concatenate(
            [
                to_16(weights[b * step : (b + 1) * step]),
                to_16(jnp.concatenate([pos[:half], pos[half:]], axis=1)),
                vectors if b == 0 else jnp.zeros_like(vectors),
            ],
            axis=0,
        ).astype(BF16)


def pack(parts, at, d_parts, grads, hidden, table, rising, falling, vectors, deps=()):
    width = hidden.shape[1]
    cols = 6 * PAIR
    rows = up_16(cols // parts) + up_16(table.shape[0] // parts // 2) + 16
    return pl.pallas_call(
        ordered(functools.partial(pack_kernel, parts), 16, deps),
        in_specs=[pl.BlockSpec(memory_space=pltpu.SMEM)]
        + [pl.BlockSpec(memory_space=pltpu.VMEM)] * 15
        + [pl.BlockSpec(memory_space=pl.ANY)] * len(deps),
        out_specs=pl.BlockSpec(memory_space=pltpu.VMEM),
        out_shape=jax.ShapeDtypeStruct((parts, rows, width), BF16),
        compiler_params=pltpu.CompilerParams(vmem_limit_bytes=32 * 2**20),
        cost_estimate=pl.CostEstimate(flops=8 * 10**9, bytes_accessed=10 * 2**20, transcendentals=0),
        name="pack",
    )(at, *d_parts, *grads, hidden, table, rising, falling, vectors, *deps)


def unpack_kernel(step, table_step, in_ref, q_ref, k_ref, v_ref, table_ref, vec_ref):
    parts = in_ref.shape[0]
    rows = up_16(step)
    weights = jnp.concatenate([in_ref[b, :rows].astype(F32)[:step] for b in range(parts)], axis=0)
    width = q_ref.shape[1]
    for i, ref in enumerate((q_ref, k_ref, v_ref)):
        ref[...] = weights[i * width : (i + 1) * width].T
    table = [in_ref[b, rows : rows + up_16(table_step)].astype(F32)[:table_step] for b in range(parts)]
    table_ref[...] = jnp.concatenate(table, axis=0)
    vec_ref[...] = in_ref[0, rows + up_16(table_step) :].astype(F32)


def unpack(whole, cols, table_rows):
    parts, _, width = whole.shape
    weight = jax.ShapeDtypeStruct((width, cols), F32)
    return pl.pallas_call(
        functools.partial(unpack_kernel, 3 * cols // parts, table_rows // parts),
        in_specs=[pl.BlockSpec(memory_space=pltpu.VMEM)],
        out_specs=[pl.BlockSpec(memory_space=pltpu.VMEM)] * 5,
        out_shape=[weight] * 3
        + [jax.ShapeDtypeStruct((table_rows, width), F32), jax.ShapeDtypeStruct((16, width), F32)],
        compiler_params=pltpu.CompilerParams(vmem_limit_bytes=32 * 2**20),
        name="unpack",
    )(whole)


def widen_kernel(in_ref, *refs):
    rows = in_ref[0].astype(F32)
    start = 0
    for ref in refs:
        ref[...] = rows[start : start + ref.shape[0]]
        start += ref.shape[0]


def widen(gathered, counts):
    parts, rows, width = gathered.shape
    return pl.pallas_call(
        widen_kernel,
        grid=(parts,),
        in_specs=[pl.BlockSpec((1, rows, width), lambda b: (b, 0, 0))],
        out_specs=[pl.BlockSpec((count, width), lambda b: (b, 0)) for count in counts],
        out_shape=[jax.ShapeDtypeStruct((parts * count, width), F32) for count in counts],
        cost_estimate=pl.CostEstimate(flops=0, bytes_accessed=6 * parts * rows * width, transcendentals=0),
        name="widen",
    )(gathered)


def swap(values, axis, mask):
    return lax.ppermute(values, axis, [(i, i ^ mask) for i in range(lax.axis_size(axis))])


def after(value, *deps):
    return lax.optimization_barrier((value, *deps))[0]


def pick(values, index, axis=0):
    return lax.dynamic_index_in_dim(values, index, axis, keepdims=False)


def bit_of(axis, mask):
    return (lax.axis_index(axis) & mask) // mask


def add_low(left, right):
    return (left.astype(F32) + right.astype(F32)).astype(BF16)


def pick_bit(values, at, low, bit):
    shape = values.shape
    cut = values.reshape(shape[:at] + (shape[at] // (2 * low), 2, low) + shape[at + 1 :])
    part = pick(cut, bit, at + 1)
    return part.reshape(shape[:at] + (shape[at] // 2,) + shape[at + 1 :])


def send_together(arrays, axis, mask):
    last = arrays[0].shape[-1]
    got = swap(jnp.concatenate([a.reshape(-1, last) for a in arrays], axis=0), axis, mask)
    parts = []
    start = 0
    for a in arrays:
        rows = a.size // last
        parts.append(got[start : start + rows].reshape(a.shape))
        start += rows
    return parts


def halve(arrays, ats, low, mask):
    bit = bit_of("dp", mask)
    theirs = send_together([pick_bit(a, at, low, 1 - bit) for a, at in zip(arrays, ats)], "dp", mask)
    return [pick_bit(a, at, low, bit) for a, at in zip(arrays, ats)], theirs


def add_all(pair):
    return [add_low(mine, theirs) for mine, theirs in zip(*pair)]


def low_sum_over(values, axis):
    mask = 1
    while mask < lax.axis_size(axis):
        values = add_low(values, swap(values, axis, mask))
        mask *= 2
    return values


def norm_parts(values):
    row_mean = jnp.mean(values, axis=-1, keepdims=True)
    centered = values - row_mean
    row_var = jnp.mean(centered * centered, axis=-1, keepdims=True)
    inverse = lax.rsqrt(row_var + NORM_EPS)
    return centered * inverse, inverse


def norm_back(grad, unit_rows, inverse, gain):
    d_unit = grad * gain
    mean_d = jnp.mean(d_unit, axis=-1, keepdims=True)
    mean_du = jnp.mean(d_unit * unit_rows, axis=-1, keepdims=True)
    return inverse * (d_unit - mean_d - unit_rows * mean_du)


def gelu_parts(values):
    cumulative = 0.5 + 0.5 * lax.erf(values * math.sqrt(0.5))
    density = jnp.exp(-0.5 * values * values) * (1.0 / math.sqrt(2.0 * math.pi))
    return values * cumulative, cumulative + values * density


def on_device(
    hidden_in,
    key_mask,
    bucket_of_offset,
    position_table,
    query_weight,
    query_bias,
    key_weight,
    key_bias,
    value_weight,
    value_bias,
    out_weight,
    out_bias,
    first_gain,
    first_shift,
    up_weight,
    up_bias,
    down_weight,
    down_bias,
    second_gain,
    second_shift,
    cotangent,
):
    tokens, width = hidden_in.shape
    width_loc = query_weight.shape[1]
    units = up_weight.shape[1]
    pairs = width_loc // PAIR
    dp_parts = lax.axis_size("dp")
    mp_parts = lax.axis_size("mp")
    dp_index = lax.axis_index("dp")
    mp_index = lax.axis_index("mp")
    share = tokens // mp_parts
    assert tokens == LEN and mp_parts == 4 and dp_parts & (dp_parts - 1) == 0
    dp_masks = [1 << b for b in range(dp_parts.bit_length() - 1)]
    others = range(1, mp_parts)

    def relative(blocks):
        return jnp.concatenate([pick(blocks, mp_index ^ s)[None] for s in range(mp_parts)], axis=0)

    def to_owners(blocks):
        return [blocks[0]] + [swap(blocks[s], "mp", s) for s in others]

    def by_owner(rows):
        blocks = rows.reshape(mp_parts, -1, rows.shape[1])
        return [pick(blocks, mp_index ^ s) for s in range(mp_parts)]

    def my_part(rows):
        count = rows.shape[0] // dp_parts
        return lax.dynamic_slice_in_dim(rows, dp_index * count, count, 0)

    out_slice = jnp.stack(to_owners([my_part(out_weight)] * mp_parts))
    bias_row = jnp.pad(up_bias.reshape(1, units), ((0, 15), (0, 0)))
    far_slice = jnp.concatenate([my_part(up_weight), my_part(down_weight), bias_row], axis=0)
    far_slice = swap(far_slice, "mp", 2)
    far_bias = far_slice[-16]

    row_two = (1, width_loc)
    falling = jnp.concatenate([bucket_of_offset[:1], bucket_of_offset[::-1]])[None, :]
    rising = jnp.concatenate([bucket_of_offset, bucket_of_offset[:1]])[None, :]
    queries, keys_all, values_all, key_rows, query_rows, query_rows_up = project(
        hidden_in,
        position_table,
        rising,
        falling,
        (query_weight, key_weight, value_weight),
        (query_bias.reshape(row_two), key_bias.reshape(row_two), value_bias.reshape(row_two)),
    )
    weight_cat = jnp.concatenate([query_weight, key_weight, value_weight], axis=1)

    out_all = jnp.swapaxes(lax.all_gather(out_slice, "dp", axis=0), 0, 1).reshape(width, width)

    probs = []
    context = []
    for pair in range(pairs):
        prob, ctx = attn_fwd(
            pair, queries, keys_all, values_all, key_rows, query_rows, key_mask.reshape(1, tokens)
        )
        probs.append(prob)
        context.append(ctx)
        if pair == 0:
            far_all = lax.all_gather(after(far_slice, ctx), "dp", axis=0)
    context = jnp.concatenate(context, axis=1)
    ctx_rows = jnp.concatenate(to_owners(by_owner(context)), axis=1)

    own_rows = lax.dynamic_slice_in_dim(hidden_in, mp_index * share, share, 0)
    pre_first = dot(ctx_rows, out_all) + out_bias.astype(F32) + own_rows.astype(F32)
    unit_first, inverse_first = norm_parts(pre_first)
    gain_first = first_gain.astype(F32)
    normed = unit_first * gain_first + first_shift.astype(F32)
    normed_low = normed.astype(BF16)

    near_low = swap(normed_low, "mp", 1)
    up_cat = jnp.concatenate([up_weight, far_all[:, : width // dp_parts].reshape(width, units)], axis=1)
    down_cat = jnp.concatenate([down_weight, far_all[:, width // dp_parts : -16].reshape(units, width)], axis=0)
    bias_cat = jnp.concatenate([up_bias, far_bias], axis=0).astype(F32)

    def feed(rows):
        act, slope = gelu_parts(dot(rows, up_cat) + bias_cat)
        act_low = act.astype(BF16)
        return act_low, slope.astype(BF16), dot(act_low, down_cat)

    act_near, slope_near, mixed_near = feed(near_low)
    mixed_near = mixed_near.astype(BF16)
    act_own, slope_own, mixed_own = feed(after(normed_low, mixed_near))
    mixed = mixed_own + swap(mixed_near, "mp", 1).astype(F32)
    pre_second = mixed + down_bias.astype(F32) + normed

    unit_second, inverse_second = norm_parts(pre_second)
    gain_second = second_gain.astype(F32)
    layer_out = (unit_second * gain_second + second_shift.astype(F32)).astype(BF16)
    cot = cotangent.astype(F32)
    d_pre_second = norm_back(cot, unit_second, inverse_second, gain_second)
    d_down = d_pre_second.astype(BF16)

    near_d_down = swap(d_down, "mp", 1)

    def feed_back(d_rows, slope):
        d_inner = (dot(d_rows, down_cat, NT) * slope.astype(F32)).astype(BF16)
        return d_inner, dot(d_inner, up_cat, NT)

    d_inner_own, back_own = feed_back(d_down, slope_own)
    d_inner_near, back_near = feed_back(after(near_d_down, d_inner_own), slope_near)
    back_near = swap(back_near.astype(BF16), "mp", 1)
    d_normed = back_own + back_near.astype(F32) + d_pre_second
    act_cat = after(jnp.concatenate([act_own, act_near], axis=0), d_down)
    d_down_cat = jnp.concatenate([d_down, near_d_down], axis=0)
    normed_cat = after(jnp.concatenate([normed_low, near_low], axis=0), d_down)
    d_inner_cat = jnp.concatenate([d_inner_own, d_inner_near], axis=0)

    half = dp_parts // 2

    def blocks_of(cols, which, groups):
        step = cols.shape[1] // (groups * dp_parts)
        return jnp.concatenate(
            [
                lax.dynamic_slice_in_dim(cols, (g * dp_parts + 2 * j + which) * step, step, 1)
                for g in range(groups)
                for j in range(half)
            ],
            axis=1,
        )

    def halves_sum(make):
        bit = bit_of("dp", 1)
        theirs = swap(make(1 - bit).astype(BF16), "dp", 1)
        return (make(bit) + theirs.astype(F32)).astype(BF16)

    down_sum = halves_sum(lambda which: dot(blocks_of(act_cat, which, 2), d_down_cat, TN))
    down_sum = down_sum.reshape(2, half, units // dp_parts, width)
    up_sum = halves_sum(lambda which: dot(blocks_of(normed_cat, which, 1), d_inner_cat, TN))
    up_sum = up_sum.reshape(half, width // dp_parts, 2 * units)
    up_bias_part = jnp.sum(d_inner_cat.astype(F32), axis=0)

    d_pre_first = norm_back(d_normed, unit_first, inverse_first, gain_first)
    d_attn = d_pre_first.astype(BF16)
    d_ctx = dot(d_attn, out_all, NT).astype(BF16)
    d_ctx_parts = jnp.stack(
        to_owners([d_ctx[:, s * width_loc : (s + 1) * width_loc] for s in range(mp_parts)])
    )
    out_sum = dot(ctx_rows, d_attn, TN).astype(BF16).reshape(mp_parts, dp_parts, -1, width)
    sums = jnp.stack(
        [
            jnp.sum(d_pre_first, axis=0),
            jnp.sum(d_normed * unit_first, axis=0),
            jnp.sum(d_normed, axis=0),
            jnp.sum(d_pre_second, axis=0),
            jnp.sum(cot * unit_second, axis=0),
            jnp.sum(cot, axis=0),
        ]
    )

    d_ctx = jnp.concatenate(
        [pick(d_ctx_parts, mp_index ^ s) for s in range(mp_parts)], axis=0
    )

    def rows_step(pair, deps):
        return attn_bwd_rows(pair, queries, keys_all, values_all, key_rows, probs[pair], d_ctx, deps)

    def cols_step(pair, deps):
        _, _, _, d_score, turned = by_rows[pair]
        return attn_bwd_cols(pair, keys_all, query_rows_up, d_score, turned, deps)

    low_bits = list(range(len(dp_masks) - 1))
    cut = max(1, len(low_bits) // 2)

    def steps(arrays, ats, bits, left):
        pair = None
        for bit in bits:
            pair = halve(arrays if pair is None else add_all(pair), ats, 1 << left.index(bit), 2 << bit)
            left.remove(bit)
        return pair

    def tied(pair, *deps):
        return pair[0], [after(theirs, *deps) for theirs in pair[1]]

    left_one, left_two = list(low_bits), list(low_bits)
    bits_one, bits_two = low_bits, low_bits[::-1]
    step_two = steps([up_sum], [0], bits_two[:cut], left_two)
    step_out = halve([out_sum], [1], 1, 1)
    step_one = steps([down_sum], [1], bits_one[:cut], left_one)
    by_rows = [rows_step(0, (up_sum, down_sum, step_out[0][0]))]
    (down_sum,) = add_all(tied(step_one, by_rows[0][1]))
    (up_sum,) = add_all(tied(step_two, by_rows[0][1]))
    (out_sum,) = add_all(tied(step_out, by_rows[0][1]))
    step_one = steps([down_sum], [1], bits_one[cut:], left_one)
    step_two = steps([up_sum], [0], bits_two[cut:], left_two)
    step_out = steps([out_sum], [1], bits_one[:cut], list(low_bits))
    by_rows.append(rows_step(1, (by_rows[0][1], down_sum, up_sum, out_sum)))
    d_query, d_value = (jnp.concatenate([r[i] for r in by_rows], axis=1) for i in (0, 1))
    key_grad = jnp.concatenate([r[2] for r in by_rows], axis=0)
    d_value1 = by_rows[1][1]
    (down_sum,) = add_all(tied(step_one, d_value1))
    (up_sum,) = add_all(tied(step_two, d_value1))
    (out_sum,) = add_all(tied(step_out, d_value1))
    step_out = steps([out_sum], [1], bits_one[cut:], low_bits[cut:])
    down_sum, up_sum = down_sum[:, 0], up_sum[0]
    down_rows = down_sum.shape[1]
    far = send_together([down_sum[1], up_sum[:, units:]], "mp", 2)
    by_cols = [cols_step(0, (down_sum, up_sum, out_sum))]
    (out_sum,) = add_all(tied(step_out, by_cols[0][0]))
    out_sum = out_sum[:, 0]
    out_rows = out_sum.shape[1]
    by_cols.append(cols_step(1, (by_cols[0][0], out_sum)))
    d_key = jnp.concatenate([r[0] for r in by_cols], axis=1)
    query_grad = jnp.concatenate([r[1] for r in by_cols], axis=0)
    out_parts = to_owners([out_sum[s] for s in range(mp_parts)])
    out_sum = out_parts[0].astype(F32) + sum(after(p, d_key).astype(F32) for p in out_parts[1:])
    far = [after(part, d_key) for part in far]
    ready = jnp.concatenate(
        [
            add_low(down_sum[0], far[0]),
            add_low(up_sum[:, :units], far[1]),
            out_sum.astype(BF16),
        ],
        axis=0,
    )
    gathered = lax.all_gather(ready, "dp", axis=0)
    d_cat = after(jnp.concatenate([d_query, d_key, d_value], axis=1), ready)
    input_low = dot(d_cat, weight_cat, NT).astype(BF16)
    input_part = lax.psum_scatter(after(input_low, gathered), "mp", scatter_dimension=0, tiled=True)
    input_grad = d_pre_first + input_part.astype(F32)

    d_key1 = after(by_cols[1][0], input_low)

    device_ids = jnp.arange(mp_parts)[:, None]
    up_bias_part = jnp.where(device_ids == mp_index, up_bias_part[:units], 0.0) + jnp.where(
        device_ids == (mp_index ^ 2), up_bias_part[units:], 0.0
    )
    vectors = jnp.concatenate([jnp.zeros_like(up_bias_part), sums, up_bias_part], axis=0)
    vectors = jnp.pad(vectors, ((0, 16 - vectors.shape[0]), (0, 0)))
    message = pack(
        dp_parts,
        mp_index.reshape(1),
        [by_rows[0][0], by_rows[1][0], by_cols[0][0], d_key1, by_rows[0][1], by_rows[1][1]],
        [by_cols[0][1], by_cols[1][1], by_rows[0][2], by_rows[1][2]],
        hidden_in,
        position_table,
        rising,
        falling,
        vectors,
    )

    (message,) = add_all(halve([message], [0], 1, 1))
    block_index = dp_index // 2
    total = pick(message, block_index).astype(F32)
    for s in range(1, half):
        total = total + swap(pick(message, block_index ^ s), "dp", 2 * s).astype(F32)
    down_weight_grad, up_weight_grad, out_weight_grad = widen(gathered, (down_rows, down_rows, out_rows))
    step = 3 * width_loc // dp_parts
    table_rows = position_table.shape[0]
    table_step = table_rows // dp_parts
    packed = total[up_16(step) : up_16(step) + table_step // 2].astype(BF16)
    packed = jnp.concatenate([packed[:, : 2 * width_loc], packed[:, 2 * width_loc :]], axis=0)
    table_part = dot(packed, weight_cat[:, : 2 * width_loc], NT)
    shared_sum = jnp.concatenate([to_16(table_part), total[-16:]], axis=0).astype(BF16)
    shared_sum = low_sum_over(shared_sum, "mp")
    block = jnp.concatenate([total[: up_16(step)].astype(BF16), shared_sum], axis=0)
    parts = jnp.stack([block] + [swap(block, "dp", 2 * s) for s in range(1, half)])
    mine = jnp.stack([pick(parts, block_index ^ j) for j in range(half)])
    mine = after(mine, down_weight_grad)
    theirs = swap(mine, "dp", 1)
    even = bit_of("dp", 1) == 0
    whole = jnp.stack([jnp.where(even, mine, theirs), jnp.where(even, theirs, mine)], axis=1)
    whole = whole.reshape(dp_parts, -1, width)
    query_weight_grad, key_weight_grad, value_weight_grad, table_grad, vectors = unpack(
        whole, width_loc, table_rows
    )
    biases = lax.dynamic_index_in_dim(vectors, mp_index, 0, keepdims=False)
    query_bias_grad, key_bias_grad, value_bias_grad = (
        biases[i * width_loc : (i + 1) * width_loc] for i in range(3)
    )
    shared_sums = vectors[mp_parts:]
    up_bias_grad = lax.dynamic_index_in_dim(vectors, mp_parts + 6 + mp_index, 0, keepdims=False)

    out_bias_grad, first_gain_grad, first_shift_grad, down_bias_grad, second_gain_grad, second_shift_grad = (
        shared_sums[i] for i in range(6)
    )
    return (
        layer_out,
        input_grad,
        table_grad,
        query_weight_grad,
        query_bias_grad,
        key_weight_grad,
        key_bias_grad,
        value_weight_grad,
        value_bias_grad,
        out_weight_grad,
        out_bias_grad,
        first_gain_grad,
        first_shift_grad,
        up_weight_grad,
        up_bias_grad,
        down_weight_grad,
        down_bias_grad,
        second_gain_grad,
        second_shift_grad,
    )


def solution(mesh):
    return jax.shard_map(
        on_device,
        mesh=mesh,
        in_specs=(
            P("dp", None),
            P("dp"),
            P(),
            P(),
            P(None, "mp"),
            P("mp"),
            P(None, "mp"),
            P("mp"),
            P(None, "mp"),
            P("mp"),
            P("mp", None),
            P(),
            P(),
            P(),
            P(None, "mp"),
            P("mp"),
            P("mp", None),
            P(),
            P(),
            P(),
            P(("dp", "mp"), None),
        ),
        out_specs=(
            P(("dp", "mp"), None),
            P(("dp", "mp"), None),
            P(),
            P(None, "mp"),
            P("mp"),
            P(None, "mp"),
            P("mp"),
            P(None, "mp"),
            P("mp"),
            P("mp", None),
            P(),
            P(),
            P(),
            P(None, "mp"),
            P("mp"),
            P("mp", None),
            P(),
            P(),
            P(),
        ),
        check_vma=False,
    )
```

```python
import functools
import math

import jax
import jax.numpy as jnp
from jax import lax
from jax.experimental import pallas as pl
from jax.experimental.pallas import tpu as pltpu
from jax.sharding import PartitionSpec as P

HEAD = 64
PAIR = 2 * HEAD
LEN = 1024
BLK = 256

NORM_EPS = 1e-07
MASK_FILL = -1000000000.0
SCALE = 1.0 / math.sqrt(3.0 * HEAD)

F32 = jnp.float32
BF16 = jnp.bfloat16

NN = (((1,), (0,)), ((), ()))
NT = (((1,), (1,)), ((), ()))
TN = (((0,), (0,)), ((), ()))


def dot(left, right, dims=NN):
    return lax.dot_general(left, right, dims, preferred_element_type=F32)


def ordered(kernel, inputs, deps):
    def body(*refs):
        kernel(*refs[:inputs], *refs[inputs + len(deps) :])

    return body


def half_of(values, half):
    lane = lax.broadcasted_iota(jnp.int32, (1, PAIR), 1)
    return jnp.where((lane >= HEAD) if half else (lane < HEAD), values, jnp.zeros_like(values))


def join_halves(first, second):
    lane = lax.broadcasted_iota(jnp.int32, (1, PAIR), 1)
    return jnp.where(lane < HEAD, first, second)


def unit_matrix(flipped):
    row = lax.broadcasted_iota(jnp.int32, (BLK, BLK), 0)
    col = lax.broadcasted_iota(jnp.int32, (BLK, BLK), 1)
    hit = (row + col == BLK - 1) if flipped else (row == col)
    return hit.astype(F32).astype(BF16)


def shear(values):
    return pltpu.roll(values, 0, 1, stride=1, stride_axis=0)[:, BLK:]


def spread(values, base):
    wide = jnp.concatenate([values, jnp.zeros((values.shape[0], BLK), values.dtype)], axis=1)
    return pltpu.roll(wide, base, 1, stride=1, stride_axis=0)


def project_kernel(hidden_ref, table_ref, rising_ref, falling_ref, *refs):
    weights, biases, outs = refs[:3], refs[3:6], refs[6:]
    table_rows = table_ref.shape[0]
    bucket = lax.broadcasted_iota(jnp.int32, (table_rows, rising_ref.shape[1]), 0)
    falling = (bucket == falling_ref[...]).astype(F32).astype(BF16)
    positions = []
    for i in range(3):
        bias = biases[i][...].astype(F32)
        if i < 2:
            positions.append((dot(table_ref[...], weights[i][...]) + bias).astype(BF16))
        outs[i][...] = (dot(hidden_ref[...], weights[i][...]) + bias).astype(BF16)
    outs[3][...] = dot(positions[1], falling, TN).astype(BF16)
    outs[4][...] = dot(positions[0], falling, TN).astype(BF16)
    rising = (bucket == rising_ref[...]).astype(F32).astype(BF16)
    outs[5][...] = dot(positions[0], rising, TN).astype(BF16)


def project(hidden, table, rising, falling, weights, biases):
    tokens = hidden.shape[0]
    width = weights[0].shape[1]
    operands = (hidden, table, rising, falling, *weights, *biases)
    outs = [jax.ShapeDtypeStruct((tokens, width), BF16)] * 3
    outs += [jax.ShapeDtypeStruct((width, rising.shape[1]), BF16)] * 3

    def full(array):
        return pl.BlockSpec(array.shape, lambda i: (0,) * len(array.shape))

    return pl.pallas_call(
        project_kernel,
        grid=(1,),
        in_specs=[full(array) for array in operands],
        out_specs=[full(array) for array in outs],
        out_shape=outs,
        compiler_params=pltpu.CompilerParams(vmem_limit_bytes=40 * 2**20),
        cost_estimate=pl.CostEstimate(flops=6 * 10**9, bytes_accessed=8 * 2**20, transcendentals=0),
        name="project",
    )(*operands)


def fwd_kernel(q_ref, k_ref, v_ref, kr_ref, qr_ref, mask_ref, p_ref, ctx_ref, from_scr):
    length = k_ref.shape[0]
    span = length + BLK
    step = pl.program_id(0)

    @pl.when(step == 0)
    def _():
        def from_rows(b, carry):
            j0 = pl.multiple_of(b * BLK, BLK)
            slab = qr_ref[:, pl.ds(pl.multiple_of(length - BLK - j0, BLK), span)]
            kb = k_ref[pl.ds(j0, BLK), :]
            for half in (0, 1):
                part = dot(half_of(kb, half), slab)
                from_scr[half, pl.ds(j0, BLK), :] = shear(part).astype(BF16)
            return carry

        lax.fori_loop(0, length // BLK, from_rows, 0)

    ident = unit_matrix(False)
    live = mask_ref[...] > 0
    i0 = pl.multiple_of(step * BLK, BLK)
    slab = kr_ref[:, pl.ds(pl.multiple_of(length - BLK - i0, BLK), span)]
    qb = q_ref[pl.ds(i0, BLK), :]
    parts = []
    for half in (0, 1):
        qm = half_of(qb, half)
        to_pos = shear(dot(qm, slab))
        left = jnp.concatenate([ident, qm], axis=1)
        right = jnp.concatenate([from_scr[half, :, pl.ds(i0, BLK)], k_ref[...]], axis=1)
        score = (dot(left, right, NT) + to_pos) * SCALE
        score = jnp.where(live, score, MASK_FILL)
        expd = jnp.exp(score - jnp.max(score, axis=1, keepdims=True))
        prob = (expd * (1.0 / jnp.sum(expd, axis=1, keepdims=True))).astype(BF16)
        p_ref[half] = prob
        parts.append(dot(prob, v_ref[...]))
    ctx_ref[...] = join_halves(parts[0], parts[1]).astype(BF16)


def attn_fwd(pair, q, k, v, kr, qr, mask, deps=()):
    length = q.shape[0]
    col = pl.BlockSpec((length, PAIR), lambda i: (0, pair))
    rows = pl.BlockSpec((PAIR, 2 * length), lambda i: (pair, 0))
    return pl.pallas_call(
        ordered(fwd_kernel, 6, deps),
        grid=(length // BLK,),
        in_specs=[col, col, col, rows, rows, pl.BlockSpec((1, length), lambda i: (0, 0))]
        + [pl.BlockSpec(memory_space=pl.ANY)] * len(deps),
        out_specs=[
            pl.BlockSpec((2, BLK, length), lambda i: (0, i, 0)),
            pl.BlockSpec((BLK, PAIR), lambda i: (i, 0)),
        ],
        out_shape=[
            pltpu.HBM((2, length, length), BF16),
            jax.ShapeDtypeStruct((length, PAIR), BF16),
        ],
        scratch_shapes=[pltpu.VMEM((2, length, length), BF16)],
        compiler_params=pltpu.CompilerParams(vmem_limit_bytes=20 * 2**20),
        cost_estimate=pl.CostEstimate(
            flops=128 * length * length * PAIR, bytes_accessed=10 * 2**20, transcendentals=2 * length * length
        ),
        name="attn_fwd",
    )(q, k, v, kr, qr, mask, *deps)


def bwd_rows_kernel(
    q_ref, k_ref, v_ref, kr_ref, p_ref, dc_ref, dq_ref, dv_ref, dkr_ref, ds_ref, qrev_ref, dv_scr, dkr_scr
):
    length = k_ref.shape[0]
    span = length + BLK
    step = pl.program_id(0)
    last = pl.num_programs(0) - 1

    @pl.when(step == 0)
    def _():
        dv_scr[...] = jnp.zeros_like(dv_scr)
        dkr_scr[...] = jnp.zeros_like(dkr_scr)

    rev = unit_matrix(True)
    i0 = pl.multiple_of(step * BLK, BLK)
    u0 = pl.multiple_of(length - BLK - i0, BLK)
    slab = kr_ref[:, pl.ds(u0, span)]
    qb = dot(rev, q_ref[pl.ds(i0, BLK), :]).astype(BF16)
    qrev_ref[...] = qb
    dcb = dc_ref[pl.ds(i0, BLK), :]
    dcr = dot(rev, dcb).astype(BF16)
    parts = []
    dv_part = 0.0
    dkr_part = 0.0
    for half in (0, 1):
        prob = p_ref[half]
        d_prob = dot(half_of(dcr, half), v_ref[...], NT)
        prob_rev = dot(rev, prob)
        weighted = prob_rev * d_prob
        d_score = weighted - prob_rev * jnp.sum(weighted, axis=1, keepdims=True)
        d_low = d_score.astype(BF16)
        ds_ref[half] = d_low
        d_to = spread(d_score, 1).astype(BF16)
        parts.append(dot(d_low, k_ref[...]) + dot(d_to, slab, NT))
        dv_part = dv_part + dot(half_of(dcb, half), prob, TN)
        dkr_part = dkr_part + dot(half_of(qb, half), d_to, TN)
    dqb = (join_halves(parts[0], parts[1]) * SCALE).astype(BF16)
    dq_ref[...] = dot(rev, dqb).astype(BF16)
    dv_scr[...] += dv_part
    dkr_scr[:, pl.ds(u0, span)] += dkr_part

    @pl.when(step == last)
    def _():
        dv_ref[...] = dv_scr[...].T.astype(BF16)
        dkr_ref[...] = (dkr_scr[...] * SCALE).astype(BF16)


def attn_bwd_rows(pair, q, k, v, kr, p, dc, deps=()):
    length = q.shape[0]
    steps = length // BLK
    col = pl.BlockSpec((length, PAIR), lambda i: (0, pair))
    whole = pl.BlockSpec((length, PAIR), lambda i: (0, 0))
    turned = pl.BlockSpec((BLK, PAIR), lambda i: (steps - 1 - i, 0))
    cols = jax.ShapeDtypeStruct((length, PAIR), BF16)
    return pl.pallas_call(
        ordered(bwd_rows_kernel, 6, deps),
        grid=(steps,),
        in_specs=[
            col,
            col,
            col,
            pl.BlockSpec((PAIR, 2 * length), lambda i: (pair, 0)),
            pl.BlockSpec((2, BLK, length), lambda i: (0, i, 0)),
            col,
        ]
        + [pl.BlockSpec(memory_space=pl.ANY)] * len(deps),
        out_specs=[
            pl.BlockSpec((BLK, PAIR), lambda i: (i, 0)),
            whole,
            pl.BlockSpec((PAIR, 2 * length), lambda i: (0, 0)),
            pl.BlockSpec((2, BLK, length), lambda i: (0, steps - 1 - i, 0)),
            turned,
        ],
        out_shape=[
            cols,
            cols,
            jax.ShapeDtypeStruct((PAIR, 2 * length), BF16),
            pltpu.HBM((2, length, length), BF16),
            cols,
        ],
        scratch_shapes=[pltpu.VMEM((PAIR, length), F32), pltpu.VMEM((PAIR, 2 * length), F32)],
        compiler_params=pltpu.CompilerParams(vmem_limit_bytes=20 * 2**20),
        cost_estimate=pl.CostEstimate(
            flops=128 * length * length * PAIR, bytes_accessed=10 * 2**20, transcendentals=0
        ),
        name="attn_bwd_rows",
    )(q, k, v, kr, p, dc, *deps)


def bwd_cols_kernel(k_ref, qr_ref, ds_ref, qrev_ref, dk_ref, dqr_ref, dqr_scr):
    length = k_ref.shape[0]
    span = length + BLK
    step = pl.program_id(0)
    last = pl.num_programs(0) - 1

    @pl.when(step == 0)
    def _():
        dqr_scr[...] = jnp.zeros_like(dqr_scr)

    ident = unit_matrix(False)
    j0 = pl.multiple_of(step * BLK, BLK)
    slab = qr_ref[:, pl.ds(j0, span)]
    kb = k_ref[pl.ds(j0, BLK), :]
    parts = []
    dqr_part = 0.0
    for half in (0, 1):
        turned = dot(ident, ds_ref[half], NT)
        d_from = spread(turned, 0).astype(BF16)
        parts.append(dot(turned.astype(BF16), qrev_ref[...]) + dot(d_from, slab, NT))
        dqr_part = dqr_part + dot(half_of(kb, half), d_from, TN)
    dk_ref[...] = (join_halves(parts[0], parts[1]) * SCALE).astype(BF16)
    dqr_scr[:, pl.ds(j0, span)] += dqr_part

    @pl.when(step == last)
    def _():
        dqr_ref[...] = (dqr_scr[...] * SCALE).astype(BF16)


def attn_bwd_cols(pair, k, qr, ds, qrev, deps=()):
    length = k.shape[0]
    return pl.pallas_call(
        ordered(bwd_cols_kernel, 4, deps),
        grid=(length // BLK,),
        in_specs=[
            pl.BlockSpec((length, PAIR), lambda i: (0, pair)),
            pl.BlockSpec((PAIR, 2 * length), lambda i: (pair, 0)),
            pl.BlockSpec((2, length, BLK), lambda i: (0, 0, i)),
            pl.BlockSpec((length, PAIR), lambda i: (0, 0)),
        ]
        + [pl.BlockSpec(memory_space=pl.ANY)] * len(deps),
        out_specs=[
            pl.BlockSpec((BLK, PAIR), lambda i: (i, 0)),
            pl.BlockSpec((PAIR, 2 * length), lambda i: (0, 0)),
        ],
        out_shape=[
            jax.ShapeDtypeStruct((length, PAIR), BF16),
            jax.ShapeDtypeStruct((PAIR, 2 * length), BF16),
        ],
        scratch_shapes=[pltpu.VMEM((PAIR, 2 * length), F32)],
        compiler_params=pltpu.CompilerParams(vmem_limit_bytes=20 * 2**20),
        cost_estimate=pl.CostEstimate(
            flops=88 * length * length * PAIR, bytes_accessed=10 * 2**20, transcendentals=0
        ),
        name="attn_bwd_cols",
    )(k, qr, ds, qrev, *deps)


def to_16(rows):
    more = -rows.shape[0] % 16
    if more:
        rows = jnp.concatenate([rows, jnp.zeros((more, rows.shape[1]), rows.dtype)], axis=0)
    return rows


def up_16(count):
    return count + -count % 16


def pack_kernel(parts, at_ref, *refs):
    d_refs, g_refs = refs[:6], refs[6:10]
    hidden_ref, table_ref, rising_ref, falling_ref, vec_ref, out_ref = refs[10:]
    table_rows = table_ref.shape[0]
    length = rising_ref.shape[1]
    bucket = lax.broadcasted_iota(jnp.int32, (table_rows, length), 0)
    weights = []
    positions = []
    biases = []
    for which in range(3):
        d_both = jnp.concatenate([d_refs[2 * which][...], d_refs[2 * which + 1][...]], axis=1)
        grad = dot(d_both, hidden_ref[...], TN)
        bias = jnp.sum(d_both.astype(F32), axis=0, keepdims=True)
        if which < 2:
            index_ref = (rising_ref, falling_ref)[which]
            hot = (bucket == index_ref[...]).astype(F32).astype(BF16)
            rows = jnp.concatenate([g_refs[2 * which][...], g_refs[2 * which + 1][...]], axis=0)
            pos = dot(hot, rows, NT)
            bias = bias + jnp.sum(pos, axis=0, keepdims=True)
            grad = grad + dot(pos.astype(BF16), table_ref[...], TN)
            positions.append(pos)
        weights.append(grad)
        biases.append(bias)
    weights = jnp.concatenate(weights, axis=0)
    positions = jnp.concatenate(positions, axis=1)
    width = weights.shape[1]
    biases = jnp.concatenate(biases, axis=1)
    biases = jnp.concatenate([biases, jnp.zeros((1, width - biases.shape[1]), F32)], axis=1)
    mine = lax.broadcasted_iota(jnp.int32, (16, width), 0) == at_ref[0]
    vectors = vec_ref[...] + jnp.where(mine, biases, 0.0)
    step = weights.shape[0] // parts
    half = table_rows // parts // 2
    for b in range(parts):
        pos = positions[2 * b * half : 2 * (b + 1) * half]
        out_ref[b] = jnp.concatenate(
            [
                to_16(weights[b * step : (b + 1) * step]),
                to_16(jnp.concatenate([pos[:half], pos[half:]], axis=1)),
                vectors if b == 0 else jnp.zeros_like(vectors),
            ],
            axis=0,
        ).astype(BF16)


def pack(parts, at, d_parts, grads, hidden, table, rising, falling, vectors, deps=()):
    width = hidden.shape[1]
    cols = 6 * PAIR
    rows = up_16(cols // parts) + up_16(table.shape[0] // parts // 2) + 16
    return pl.pallas_call(
        ordered(functools.partial(pack_kernel, parts), 16, deps),
        in_specs=[pl.BlockSpec(memory_space=pltpu.SMEM)]
        + [pl.BlockSpec(memory_space=pltpu.VMEM)] * 15
        + [pl.BlockSpec(memory_space=pl.ANY)] * len(deps),
        out_specs=pl.BlockSpec(memory_space=pltpu.VMEM),
        out_shape=jax.ShapeDtypeStruct((parts, rows, width), BF16),
        compiler_params=pltpu.CompilerParams(vmem_limit_bytes=32 * 2**20),
        cost_estimate=pl.CostEstimate(flops=8 * 10**9, bytes_accessed=10 * 2**20, transcendentals=0),
        name="pack",
    )(at, *d_parts, *grads, hidden, table, rising, falling, vectors, *deps)


def unpack_kernel(step, table_step, in_ref, q_ref, k_ref, v_ref, table_ref, vec_ref):
    parts = in_ref.shape[0]
    rows = up_16(step)
    weights = jnp.concatenate([in_ref[b, :rows].astype(F32)[:step] for b in range(parts)], axis=0)
    width = q_ref.shape[1]
    for i, ref in enumerate((q_ref, k_ref, v_ref)):
        ref[...] = weights[i * width : (i + 1) * width].T
    table = [in_ref[b, rows : rows + up_16(table_step)].astype(F32)[:table_step] for b in range(parts)]
    table_ref[...] = jnp.concatenate(table, axis=0)
    vec_ref[...] = in_ref[0, rows + up_16(table_step) :].astype(F32)


def unpack(whole, cols, table_rows):
    parts, _, width = whole.shape
    weight = jax.ShapeDtypeStruct((width, cols), F32)
    return pl.pallas_call(
        functools.partial(unpack_kernel, 3 * cols // parts, table_rows // parts),
        in_specs=[pl.BlockSpec(memory_space=pltpu.VMEM)],
        out_specs=[pl.BlockSpec(memory_space=pltpu.VMEM)] * 5,
        out_shape=[weight] * 3
        + [jax.ShapeDtypeStruct((table_rows, width), F32), jax.ShapeDtypeStruct((16, width), F32)],
        compiler_params=pltpu.CompilerParams(vmem_limit_bytes=32 * 2**20),
        name="unpack",
    )(whole)


def widen_kernel(in_ref, *refs):
    rows = in_ref[0].astype(F32)
    start = 0
    for ref in refs:
        ref[...] = rows[start : start + ref.shape[0]]
        start += ref.shape[0]


def widen(gathered, counts):
    parts, rows, width = gathered.shape
    return pl.pallas_call(
        widen_kernel,
        grid=(parts,),
        in_specs=[pl.BlockSpec((1, rows, width), lambda b: (b, 0, 0))],
        out_specs=[pl.BlockSpec((count, width), lambda b: (b, 0)) for count in counts],
        out_shape=[jax.ShapeDtypeStruct((parts * count, width), F32) for count in counts],
        cost_estimate=pl.CostEstimate(flops=0, bytes_accessed=6 * parts * rows * width, transcendentals=0),
        name="widen",
    )(gathered)


def swap(values, axis, mask):
    return lax.ppermute(values, axis, [(i, i ^ mask) for i in range(lax.axis_size(axis))])


def after(value, *deps):
    return lax.optimization_barrier((value, *deps))[0]


def pick(values, index, axis=0):
    return lax.dynamic_index_in_dim(values, index, axis, keepdims=False)


def bit_of(axis, mask):
    return (lax.axis_index(axis) & mask) // mask


def add_low(left, right):
    return (left.astype(F32) + right.astype(F32)).astype(BF16)


def pick_bit(values, at, low, bit):
    shape = values.shape
    cut = values.reshape(shape[:at] + (shape[at] // (2 * low), 2, low) + shape[at + 1 :])
    part = pick(cut, bit, at + 1)
    return part.reshape(shape[:at] + (shape[at] // 2,) + shape[at + 1 :])


def send_together(arrays, axis, mask):
    last = arrays[0].shape[-1]
    got = swap(jnp.concatenate([a.reshape(-1, last) for a in arrays], axis=0), axis, mask)
    parts = []
    start = 0
    for a in arrays:
        rows = a.size // last
        parts.append(got[start : start + rows].reshape(a.shape))
        start += rows
    return parts


def halve(arrays, ats, low, mask):
    bit = bit_of("dp", mask)
    theirs = send_together([pick_bit(a, at, low, 1 - bit) for a, at in zip(arrays, ats)], "dp", mask)
    return [pick_bit(a, at, low, bit) for a, at in zip(arrays, ats)], theirs


def add_all(pair):
    return [add_low(mine, theirs) for mine, theirs in zip(*pair)]


def low_sum_over(values, axis, beside):
    mask = 1
    while mask < lax.axis_size(axis):
        values = add_low(values, swap(values, axis, mask))
        if mask == 1:
            values = after(values, beside)
        mask *= 2
    return values


def norm_parts(values):
    row_mean = jnp.mean(values, axis=-1, keepdims=True)
    centered = values - row_mean
    row_var = jnp.mean(centered * centered, axis=-1, keepdims=True)
    inverse = lax.rsqrt(row_var + NORM_EPS)
    return centered * inverse, inverse


def norm_back(grad, unit_rows, inverse, gain):
    d_unit = grad * gain
    mean_d = jnp.mean(d_unit, axis=-1, keepdims=True)
    mean_du = jnp.mean(d_unit * unit_rows, axis=-1, keepdims=True)
    return inverse * (d_unit - mean_d - unit_rows * mean_du)


def gelu_parts(values):
    cumulative = 0.5 + 0.5 * lax.erf(values * math.sqrt(0.5))
    density = jnp.exp(-0.5 * values * values) * (1.0 / math.sqrt(2.0 * math.pi))
    return values * cumulative, cumulative + values * density


def on_device(
    hidden_in,
    key_mask,
    bucket_of_offset,
    position_table,
    query_weight,
    query_bias,
    key_weight,
    key_bias,
    value_weight,
    value_bias,
    out_weight,
    out_bias,
    first_gain,
    first_shift,
    up_weight,
    up_bias,
    down_weight,
    down_bias,
    second_gain,
    second_shift,
    cotangent,
):
    tokens, width = hidden_in.shape
    width_loc = query_weight.shape[1]
    units = up_weight.shape[1]
    pairs = width_loc // PAIR
    dp_parts = lax.axis_size("dp")
    mp_parts = lax.axis_size("mp")
    dp_index = lax.axis_index("dp")
    mp_index = lax.axis_index("mp")
    share = tokens // mp_parts
    assert tokens == LEN and mp_parts == 4 and dp_parts & (dp_parts - 1) == 0
    dp_masks = [1 << b for b in range(dp_parts.bit_length() - 1)]
    others = range(1, mp_parts)

    def relative(blocks):
        return jnp.concatenate([pick(blocks, mp_index ^ s)[None] for s in range(mp_parts)], axis=0)

    def to_owners(blocks):
        return [blocks[0]] + [swap(blocks[s], "mp", s) for s in others]

    def by_owner(rows):
        blocks = rows.reshape(mp_parts, -1, rows.shape[1])
        return [pick(blocks, mp_index ^ s) for s in range(mp_parts)]

    def my_part(rows):
        count = rows.shape[0] // dp_parts
        return lax.dynamic_slice_in_dim(rows, dp_index * count, count, 0)

    out_slice = jnp.stack(to_owners([my_part(out_weight)] * mp_parts))
    bias_row = jnp.pad(up_bias.reshape(1, units), ((0, 15), (0, 0)))
    far_slice = jnp.concatenate([my_part(up_weight), my_part(down_weight), bias_row], axis=0)
    far_slice = swap(far_slice, "mp", 2)
    far_bias = far_slice[-16]

    row_two = (1, width_loc)
    falling = jnp.concatenate([bucket_of_offset[:1], bucket_of_offset[::-1]])[None, :]
    rising = jnp.concatenate([bucket_of_offset, bucket_of_offset[:1]])[None, :]
    queries, keys_all, values_all, key_rows, query_rows, query_rows_up = project(
        hidden_in,
        position_table,
        rising,
        falling,
        (query_weight, key_weight, value_weight),
        (query_bias.reshape(row_two), key_bias.reshape(row_two), value_bias.reshape(row_two)),
    )
    weight_cat = jnp.concatenate([query_weight, key_weight, value_weight], axis=1)

    out_all = jnp.swapaxes(lax.all_gather(out_slice, "dp", axis=0), 0, 1).reshape(width, width)

    probs = []
    context = []
    for pair in range(pairs):
        prob, ctx = attn_fwd(
            pair, queries, keys_all, values_all, key_rows, query_rows, key_mask.reshape(1, tokens)
        )
        probs.append(prob)
        context.append(ctx)
        if pair == 0:
            far_all = lax.all_gather(after(far_slice, ctx), "dp", axis=0)
    context = jnp.concatenate(context, axis=1)
    ctx_rows = jnp.concatenate(to_owners(by_owner(context)), axis=1)

    own_rows = lax.dynamic_slice_in_dim(hidden_in, mp_index * share, share, 0)
    pre_first = dot(ctx_rows, out_all) + out_bias.astype(F32) + own_rows.astype(F32)
    unit_first, inverse_first = norm_parts(pre_first)
    gain_first = first_gain.astype(F32)
    normed = unit_first * gain_first + first_shift.astype(F32)
    normed_low = normed.astype(BF16)

    near_low = swap(normed_low, "mp", 1)
    up_cat = jnp.concatenate([up_weight, far_all[:, : width // dp_parts].reshape(width, units)], axis=1)
    down_cat = jnp.concatenate([down_weight, far_all[:, width // dp_parts : -16].reshape(units, width)], axis=0)
    bias_cat = jnp.concatenate([up_bias, far_bias], axis=0).astype(F32)

    def feed(rows):
        act, slope = gelu_parts(dot(rows, up_cat) + bias_cat)
        act_low = act.astype(BF16)
        return act_low, slope.astype(BF16), dot(act_low, down_cat)

    act_near, slope_near, mixed_near = feed(near_low)
    mixed_near = mixed_near.astype(BF16)
    act_own, slope_own, mixed_own = feed(after(normed_low, mixed_near))
    mixed = mixed_own + swap(mixed_near, "mp", 1).astype(F32)
    pre_second = mixed + down_bias.astype(F32) + normed

    unit_second, inverse_second = norm_parts(pre_second)
    gain_second = second_gain.astype(F32)
    layer_out = (unit_second * gain_second + second_shift.astype(F32)).astype(BF16)
    cot = cotangent.astype(F32)
    d_pre_second = norm_back(cot, unit_second, inverse_second, gain_second)
    d_down = d_pre_second.astype(BF16)

    near_d_down = swap(d_down, "mp", 1)

    def feed_back(d_rows, slope):
        d_inner = (dot(d_rows, down_cat, NT) * slope.astype(F32)).astype(BF16)
        return d_inner, dot(d_inner, up_cat, NT)

    d_inner_own, back_own = feed_back(d_down, slope_own)
    d_inner_near, back_near = feed_back(after(near_d_down, d_inner_own), slope_near)
    back_near = swap(back_near.astype(BF16), "mp", 1)
    d_normed = back_own + back_near.astype(F32) + d_pre_second
    act_cat = after(jnp.concatenate([act_own, act_near], axis=0), d_down)
    d_down_cat = jnp.concatenate([d_down, near_d_down], axis=0)
    normed_cat = after(jnp.concatenate([normed_low, near_low], axis=0), d_down)
    d_inner_cat = jnp.concatenate([d_inner_own, d_inner_near], axis=0)

    half = dp_parts // 2

    def blocks_of(cols, which, groups):
        step = cols.shape[1] // (groups * dp_parts)
        return jnp.concatenate(
            [
                lax.dynamic_slice_in_dim(cols, (g * dp_parts + 2 * j + which) * step, step, 1)
                for g in range(groups)
                for j in range(half)
            ],
            axis=1,
        )

    def halves_sum(make):
        bit = bit_of("dp", 1)
        theirs = swap(make(1 - bit).astype(BF16), "dp", 1)
        return (make(bit) + theirs.astype(F32)).astype(BF16)

    down_sum = halves_sum(lambda which: dot(blocks_of(act_cat, which, 2), d_down_cat, TN))
    down_sum = down_sum.reshape(2, half, units // dp_parts, width)
    up_sum = halves_sum(lambda which: dot(blocks_of(normed_cat, which, 1), d_inner_cat, TN))
    up_sum = up_sum.reshape(half, width // dp_parts, 2 * units)
    up_bias_part = jnp.sum(d_inner_cat.astype(F32), axis=0)

    d_pre_first = norm_back(d_normed, unit_first, inverse_first, gain_first)
    d_attn = d_pre_first.astype(BF16)
    d_ctx = dot(d_attn, out_all, NT).astype(BF16)
    d_ctx_parts = jnp.stack(
        to_owners([d_ctx[:, s * width_loc : (s + 1) * width_loc] for s in range(mp_parts)])
    )
    out_sum = dot(ctx_rows, d_attn, TN).astype(BF16).reshape(mp_parts, dp_parts, -1, width)
    sums = jnp.stack(
        [
            jnp.sum(d_pre_first, axis=0),
            jnp.sum(d_normed * unit_first, axis=0),
            jnp.sum(d_normed, axis=0),
            jnp.sum(d_pre_second, axis=0),
            jnp.sum(cot * unit_second, axis=0),
            jnp.sum(cot, axis=0),
        ]
    )

    d_ctx = jnp.concatenate(
        [pick(d_ctx_parts, mp_index ^ s) for s in range(mp_parts)], axis=0
    )

    def rows_step(pair, deps):
        return attn_bwd_rows(pair, queries, keys_all, values_all, key_rows, probs[pair], d_ctx, deps)

    def cols_step(pair, deps):
        _, _, _, d_score, turned = by_rows[pair]
        return attn_bwd_cols(pair, keys_all, query_rows_up, d_score, turned, deps)

    low_bits = list(range(len(dp_masks) - 1))
    cut = max(1, len(low_bits) // 2)

    def steps(arrays, ats, bits, left):
        pair = None
        for bit in bits:
            pair = halve(arrays if pair is None else add_all(pair), ats, 1 << left.index(bit), 2 << bit)
            left.remove(bit)
        return pair

    def tied(pair, *deps):
        return pair[0], [after(theirs, *deps) for theirs in pair[1]]

    left_one, left_two = list(low_bits), list(low_bits)
    bits_one, bits_two = low_bits, low_bits[::-1]
    step_two = steps([up_sum], [0], bits_two[:cut], left_two)
    step_out = halve([out_sum], [1], 1, 1)
    step_one = steps([down_sum], [1], bits_one[:cut], left_one)
    by_rows = [rows_step(0, (up_sum, down_sum, step_out[0][0]))]
    (down_sum,) = add_all(tied(step_one, by_rows[0][1]))
    (up_sum,) = add_all(tied(step_two, by_rows[0][1]))
    (out_sum,) = add_all(tied(step_out, by_rows[0][1]))
    step_one = steps([down_sum], [1], bits_one[cut:], left_one)
    step_two = steps([up_sum], [0], bits_two[cut:], left_two)
    step_out = steps([out_sum], [1], bits_one[:cut], list(low_bits))
    by_rows.append(rows_step(1, (by_rows[0][1], down_sum, up_sum, out_sum)))
    d_query, d_value = (jnp.concatenate([r[i] for r in by_rows], axis=1) for i in (0, 1))
    key_grad = jnp.concatenate([r[2] for r in by_rows], axis=0)
    d_value1 = by_rows[1][1]
    (down_sum,) = add_all(tied(step_one, d_value1))
    (up_sum,) = add_all(tied(step_two, d_value1))
    (out_sum,) = add_all(tied(step_out, d_value1))
    step_out = steps([out_sum], [1], bits_one[cut:], low_bits[cut:])
    down_sum, up_sum = down_sum[:, 0], up_sum[0]
    down_rows = down_sum.shape[1]
    far = send_together([down_sum[1], up_sum[:, units:]], "mp", 2)
    by_cols = [cols_step(0, (down_sum, up_sum, out_sum))]
    (out_sum,) = add_all(tied(step_out, by_cols[0][0]))
    out_sum = out_sum[:, 0]
    out_rows = out_sum.shape[1]
    by_cols.append(cols_step(1, (by_cols[0][0], out_sum)))
    d_key = jnp.concatenate([r[0] for r in by_cols], axis=1)
    query_grad = jnp.concatenate([r[1] for r in by_cols], axis=0)
    out_parts = to_owners([out_sum[s] for s in range(mp_parts)])
    out_sum = out_parts[0].astype(F32) + sum(after(p, d_key).astype(F32) for p in out_parts[1:])
    far = [after(part, d_key) for part in far]
    ready = jnp.concatenate(
        [
            add_low(down_sum[0], far[0]),
            add_low(up_sum[:, :units], far[1]),
            out_sum.astype(BF16),
        ],
        axis=0,
    )
    gathered = lax.all_gather(ready, "dp", axis=0)
    d_cat = after(jnp.concatenate([d_query, d_key, d_value], axis=1), ready)
    input_low = dot(d_cat, weight_cat, NT).astype(BF16)
    d_key1 = after(by_cols[1][0], input_low)

    device_ids = jnp.arange(mp_parts)[:, None]
    up_bias_part = jnp.where(device_ids == mp_index, up_bias_part[:units], 0.0) + jnp.where(
        device_ids == (mp_index ^ 2), up_bias_part[units:], 0.0
    )
    vectors = jnp.concatenate([jnp.zeros_like(up_bias_part), sums, up_bias_part], axis=0)
    vectors = jnp.pad(vectors, ((0, 16 - vectors.shape[0]), (0, 0)))
    message = pack(
        dp_parts,
        mp_index.reshape(1),
        [by_rows[0][0], by_rows[1][0], by_cols[0][0], d_key1, by_rows[0][1], by_rows[1][1]],
        [by_cols[0][1], by_cols[1][1], by_rows[0][2], by_rows[1][2]],
        hidden_in,
        position_table,
        rising,
        falling,
        vectors,
    )

    (message,) = add_all(halve([message], [0], 1, 1))
    block_index = dp_index // 2

    def sum_chips(rows):
        total = pick(rows, block_index).astype(F32)
        for s in range(1, half):
            total = total + swap(pick(rows, block_index ^ s), "dp", 2 * s).astype(F32)
        return total

    down_weight_grad, up_weight_grad, out_weight_grad = widen(gathered, (down_rows, down_rows, out_rows))
    step = 3 * width_loc // dp_parts
    short = sum_chips(message[:, up_16(step) :])
    weights_sum = sum_chips(message[:, : up_16(step)]).astype(BF16)
    table_rows = position_table.shape[0]
    table_step = table_rows // dp_parts
    packed = short[: table_step // 2].astype(BF16)
    packed = jnp.concatenate([packed[:, : 2 * width_loc], packed[:, 2 * width_loc :]], axis=0)
    table_part = dot(packed, weight_cat[:, : 2 * width_loc], NT)
    shared_sum = jnp.concatenate([to_16(table_part), short[-16:]], axis=0).astype(BF16)
    shared_sum = low_sum_over(shared_sum, "mp", weights_sum)
    block = jnp.concatenate([weights_sum, shared_sum], axis=0)
    input_part = lax.psum_scatter(after(input_low, gathered, shared_sum), "mp", scatter_dimension=0, tiled=True)
    input_grad = d_pre_first + input_part.astype(F32)

    parts = jnp.stack([block] + [swap(block, "dp", 2 * s) for s in range(1, half)])
    mine = jnp.stack([pick(parts, block_index ^ j) for j in range(half)])
    theirs = swap(mine, "dp", 1)
    even = bit_of("dp", 1) == 0
    whole = jnp.stack([jnp.where(even, mine, theirs), jnp.where(even, theirs, mine)], axis=1)
    whole = whole.reshape(dp_parts, -1, width)
    query_weight_grad, key_weight_grad, value_weight_grad, table_grad, vectors = unpack(
        whole, width_loc, table_rows
    )
    biases = lax.dynamic_index_in_dim(vectors, mp_index, 0, keepdims=False)
    query_bias_grad, key_bias_grad, value_bias_grad = (
        biases[i * width_loc : (i + 1) * width_loc] for i in range(3)
    )
    shared_sums = vectors[mp_parts:]
    up_bias_grad = lax.dynamic_index_in_dim(vectors, mp_parts + 6 + mp_index, 0, keepdims=False)

    out_bias_grad, first_gain_grad, first_shift_grad, down_bias_grad, second_gain_grad, second_shift_grad = (
        shared_sums[i] for i in range(6)
    )
    return (
        layer_out,
        input_grad,
        table_grad,
        query_weight_grad,
        query_bias_grad,
        key_weight_grad,
        key_bias_grad,
        value_weight_grad,
        value_bias_grad,
        out_weight_grad,
        out_bias_grad,
        first_gain_grad,
        first_shift_grad,
        up_weight_grad,
        up_bias_grad,
        down_weight_grad,
        down_bias_grad,
        second_gain_grad,
        second_shift_grad,
    )


def solution(mesh):
    return jax.shard_map(
        on_device,
        mesh=mesh,
        in_specs=(
            P("dp", None),
            P("dp"),
            P(),
            P(),
            P(None, "mp"),
            P("mp"),
            P(None, "mp"),
            P("mp"),
            P(None, "mp"),
            P("mp"),
            P("mp", None),
            P(),
            P(),
            P(),
            P(None, "mp"),
            P("mp"),
            P("mp", None),
            P(),
            P(),
            P(),
            P(("dp", "mp"), None),
        ),
        out_specs=(
            P(("dp", "mp"), None),
            P(("dp", "mp"), None),
            P(),
            P(None, "mp"),
            P("mp"),
            P(None, "mp"),
            P("mp"),
            P(None, "mp"),
            P("mp"),
            P("mp", None),
            P(),
            P(),
            P(),
            P(None, "mp"),
            P("mp"),
            P("mp", None),
            P(),
            P(),
            P(),
        ),
        check_vma=False,
    )
```

```python
import functools
import math

import jax
import jax.numpy as jnp
from jax import lax
from jax.experimental import pallas as pl
from jax.experimental.pallas import tpu as pltpu
from jax.sharding import PartitionSpec as P

HEAD = 64
PAIR = 2 * HEAD
LEN = 1024
BLK = 256

NORM_EPS = 1e-07
MASK_FILL = -1000000000.0
SCALE = 1.0 / math.sqrt(3.0 * HEAD)

F32 = jnp.float32
BF16 = jnp.bfloat16

NN = (((1,), (0,)), ((), ()))
NT = (((1,), (1,)), ((), ()))
TN = (((0,), (0,)), ((), ()))


def dot(left, right, dims=NN):
    return lax.dot_general(left, right, dims, preferred_element_type=F32)


def ordered(kernel, inputs, deps):
    def body(*refs):
        kernel(*refs[:inputs], *refs[inputs + len(deps) :])

    return body


def half_of(values, half):
    lane = lax.broadcasted_iota(jnp.int32, (1, PAIR), 1)
    return jnp.where((lane >= HEAD) if half else (lane < HEAD), values, jnp.zeros_like(values))


def join_halves(first, second):
    lane = lax.broadcasted_iota(jnp.int32, (1, PAIR), 1)
    return jnp.where(lane < HEAD, first, second)


def unit_matrix(flipped):
    row = lax.broadcasted_iota(jnp.int32, (BLK, BLK), 0)
    col = lax.broadcasted_iota(jnp.int32, (BLK, BLK), 1)
    hit = (row + col == BLK - 1) if flipped else (row == col)
    return hit.astype(F32).astype(BF16)


def shear(values):
    return pltpu.roll(values, 0, 1, stride=1, stride_axis=0)[:, BLK:]


def spread(values, base):
    wide = jnp.concatenate([values, jnp.zeros((values.shape[0], BLK), values.dtype)], axis=1)
    return pltpu.roll(wide, base, 1, stride=1, stride_axis=0)


def project_kernel(hidden_ref, table_ref, rising_ref, falling_ref, *refs):
    weights, biases, outs = refs[:3], refs[3:6], refs[6:]
    table_rows = table_ref.shape[0]
    bucket = lax.broadcasted_iota(jnp.int32, (table_rows, rising_ref.shape[1]), 0)
    falling = (bucket == falling_ref[...]).astype(F32).astype(BF16)
    positions = []
    for i in range(3):
        bias = biases[i][...].astype(F32)
        if i < 2:
            positions.append((dot(table_ref[...], weights[i][...]) + bias).astype(BF16))
        outs[i][...] = (dot(hidden_ref[...], weights[i][...]) + bias).astype(BF16)
    outs[3][...] = dot(positions[1], falling, TN).astype(BF16)
    outs[4][...] = dot(positions[0], falling, TN).astype(BF16)
    rising = (bucket == rising_ref[...]).astype(F32).astype(BF16)
    outs[5][...] = dot(positions[0], rising, TN).astype(BF16)


def project(hidden, table, rising, falling, weights, biases):
    tokens = hidden.shape[0]
    width = weights[0].shape[1]
    operands = (hidden, table, rising, falling, *weights, *biases)
    outs = [jax.ShapeDtypeStruct((tokens, width), BF16)] * 3
    outs += [jax.ShapeDtypeStruct((width, rising.shape[1]), BF16)] * 3

    def full(array):
        return pl.BlockSpec(array.shape, lambda i: (0,) * len(array.shape))

    return pl.pallas_call(
        project_kernel,
        grid=(1,),
        in_specs=[full(array) for array in operands],
        out_specs=[full(array) for array in outs],
        out_shape=outs,
        compiler_params=pltpu.CompilerParams(vmem_limit_bytes=40 * 2**20),
        cost_estimate=pl.CostEstimate(flops=6 * 10**9, bytes_accessed=8 * 2**20, transcendentals=0),
        name="project",
    )(*operands)


def fwd_kernel(q_ref, k_ref, v_ref, kr_ref, qr_ref, mask_ref, p_ref, ctx_ref, from_scr):
    length = k_ref.shape[0]
    span = length + BLK
    step = pl.program_id(1)

    @pl.when(step == 0)
    def _():
        def from_rows(b, carry):
            j0 = pl.multiple_of(b * BLK, BLK)
            slab = qr_ref[:, pl.ds(pl.multiple_of(length - BLK - j0, BLK), span)]
            kb = k_ref[pl.ds(j0, BLK), :]
            for half in (0, 1):
                part = dot(half_of(kb, half), slab)
                from_scr[half, pl.ds(j0, BLK), :] = shear(part).astype(BF16)
            return carry

        lax.fori_loop(0, length // BLK, from_rows, 0)

    ident = unit_matrix(False)
    live = mask_ref[...] > 0
    i0 = pl.multiple_of(step * BLK, BLK)
    slab = kr_ref[:, pl.ds(pl.multiple_of(length - BLK - i0, BLK), span)]
    qb = q_ref[pl.ds(i0, BLK), :]
    parts = []
    for half in (0, 1):
        qm = half_of(qb, half)
        to_pos = shear(dot(qm, slab))
        left = jnp.concatenate([ident, qm], axis=1)
        right = jnp.concatenate([from_scr[half, :, pl.ds(i0, BLK)], k_ref[...]], axis=1)
        score = (dot(left, right, NT) + to_pos) * SCALE
        score = jnp.where(live, score, MASK_FILL)
        expd = jnp.exp(score - jnp.max(score, axis=1, keepdims=True))
        prob = (expd * (1.0 / jnp.sum(expd, axis=1, keepdims=True))).astype(BF16)
        p_ref[half] = prob
        parts.append(dot(prob, v_ref[...]))
    ctx_ref[...] = join_halves(parts[0], parts[1]).astype(BF16)


def attn_fwd(q, k, v, kr, qr, mask):
    length, width = q.shape
    col = pl.BlockSpec((length, PAIR), lambda g, i: (0, g))
    rows = pl.BlockSpec((PAIR, 2 * length), lambda g, i: (g, 0))
    return pl.pallas_call(
        fwd_kernel,
        grid=(width // PAIR, length // BLK),
        in_specs=[col, col, col, rows, rows, pl.BlockSpec((1, length), lambda g, i: (0, 0))],
        out_specs=[
            pl.BlockSpec((2, BLK, length), lambda g, i: (g, i, 0)),
            pl.BlockSpec((BLK, PAIR), lambda g, i: (i, g)),
        ],
        out_shape=[
            pltpu.HBM((width // HEAD, length, length), BF16),
            jax.ShapeDtypeStruct((length, width), BF16),
        ],
        scratch_shapes=[pltpu.VMEM((2, length, length), BF16)],
        compiler_params=pltpu.CompilerParams(vmem_limit_bytes=20 * 2**20),
        cost_estimate=pl.CostEstimate(
            flops=128 * length * length * width, bytes_accessed=20 * 2**20, transcendentals=0
        ),
        name="attn_fwd",
    )(q, k, v, kr, qr, mask)


def bwd_rows_kernel(
    q_ref, k_ref, v_ref, kr_ref, p_ref, dc_ref, dq_ref, dv_ref, dkr_ref, ds_ref, qrev_ref, dv_scr, dkr_scr
):
    length = k_ref.shape[0]
    span = length + BLK
    step = pl.program_id(0)
    last = pl.num_programs(0) - 1

    @pl.when(step == 0)
    def _():
        dv_scr[...] = jnp.zeros_like(dv_scr)
        dkr_scr[...] = jnp.zeros_like(dkr_scr)

    rev = unit_matrix(True)
    i0 = pl.multiple_of(step * BLK, BLK)
    u0 = pl.multiple_of(length - BLK - i0, BLK)
    slab = kr_ref[:, pl.ds(u0, span)]
    qb = dot(rev, q_ref[pl.ds(i0, BLK), :]).astype(BF16)
    qrev_ref[...] = qb
    dcb = dc_ref[pl.ds(i0, BLK), :]
    dcr = dot(rev, dcb).astype(BF16)
    parts = []
    dv_part = 0.0
    dkr_part = 0.0
    for half in (0, 1):
        prob = p_ref[half]
        d_prob = dot(half_of(dcr, half), v_ref[...], NT)
        prob_rev = dot(rev, prob)
        weighted = prob_rev * d_prob
        d_score = weighted - prob_rev * jnp.sum(weighted, axis=1, keepdims=True)
        d_low = d_score.astype(BF16)
        ds_ref[half] = d_low
        d_to = spread(d_score, 1).astype(BF16)
        parts.append(dot(d_low, k_ref[...]) + dot(d_to, slab, NT))
        dv_part = dv_part + dot(half_of(dcb, half), prob, TN)
        dkr_part = dkr_part + dot(half_of(qb, half), d_to, TN)
    dqb = (join_halves(parts[0], parts[1]) * SCALE).astype(BF16)
    dq_ref[...] = dot(rev, dqb).astype(BF16)
    dv_scr[...] += dv_part
    dkr_scr[:, pl.ds(u0, span)] += dkr_part

    @pl.when(step == last)
    def _():
        dv_ref[...] = dv_scr[...].T.astype(BF16)
        dkr_ref[...] = (dkr_scr[...] * SCALE).astype(BF16)


def attn_bwd_rows(pair, q, k, v, kr, p, dc, deps=()):
    length = q.shape[0]
    steps = length // BLK
    col = pl.BlockSpec((length, PAIR), lambda i: (0, pair))
    whole = pl.BlockSpec((length, PAIR), lambda i: (0, 0))
    turned = pl.BlockSpec((BLK, PAIR), lambda i: (steps - 1 - i, 0))
    cols = jax.ShapeDtypeStruct((length, PAIR), BF16)
    return pl.pallas_call(
        ordered(bwd_rows_kernel, 6, deps),
        grid=(steps,),
        in_specs=[
            col,
            col,
            col,
            pl.BlockSpec((PAIR, 2 * length), lambda i: (pair, 0)),
            pl.BlockSpec((2, BLK, length), lambda i: (pair, i, 0)),
            col,
        ]
        + [pl.BlockSpec(memory_space=pl.ANY)] * len(deps),
        out_specs=[
            pl.BlockSpec((BLK, PAIR), lambda i: (i, 0)),
            whole,
            pl.BlockSpec((PAIR, 2 * length), lambda i: (0, 0)),
            pl.BlockSpec((2, BLK, length), lambda i: (0, steps - 1 - i, 0)),
            turned,
        ],
        out_shape=[
            cols,
            cols,
            jax.ShapeDtypeStruct((PAIR, 2 * length), BF16),
            pltpu.HBM((2, length, length), BF16),
            cols,
        ],
        scratch_shapes=[pltpu.VMEM((PAIR, length), F32), pltpu.VMEM((PAIR, 2 * length), F32)],
        compiler_params=pltpu.CompilerParams(vmem_limit_bytes=20 * 2**20),
        cost_estimate=pl.CostEstimate(
            flops=128 * length * length * PAIR, bytes_accessed=10 * 2**20, transcendentals=0
        ),
        name="attn_bwd_rows",
    )(q, k, v, kr, p, dc, *deps)


def bwd_cols_kernel(k_ref, qr_ref, ds_ref, qrev_ref, dk_ref, dqr_ref, dqr_scr):
    length = k_ref.shape[0]
    span = length + BLK
    step = pl.program_id(0)
    last = pl.num_programs(0) - 1

    @pl.when(step == 0)
    def _():
        dqr_scr[...] = jnp.zeros_like(dqr_scr)

    ident = unit_matrix(False)
    j0 = pl.multiple_of(step * BLK, BLK)
    slab = qr_ref[:, pl.ds(j0, span)]
    kb = k_ref[pl.ds(j0, BLK), :]
    parts = []
    dqr_part = 0.0
    for half in (0, 1):
        turned = dot(ident, ds_ref[half], NT)
        d_from = spread(turned, 0).astype(BF16)
        parts.append(dot(turned.astype(BF16), qrev_ref[...]) + dot(d_from, slab, NT))
        dqr_part = dqr_part + dot(half_of(kb, half), d_from, TN)
    dk_ref[...] = (join_halves(parts[0], parts[1]) * SCALE).astype(BF16)
    dqr_scr[:, pl.ds(j0, span)] += dqr_part

    @pl.when(step == last)
    def _():
        dqr_ref[...] = (dqr_scr[...] * SCALE).astype(BF16)


def attn_bwd_cols(pair, k, qr, ds, qrev, deps=()):
    length = k.shape[0]
    return pl.pallas_call(
        ordered(bwd_cols_kernel, 4, deps),
        grid=(length // BLK,),
        in_specs=[
            pl.BlockSpec((length, PAIR), lambda i: (0, pair)),
            pl.BlockSpec((PAIR, 2 * length), lambda i: (pair, 0)),
            pl.BlockSpec((2, length, BLK), lambda i: (0, 0, i)),
            pl.BlockSpec((length, PAIR), lambda i: (0, 0)),
        ]
        + [pl.BlockSpec(memory_space=pl.ANY)] * len(deps),
        out_specs=[
            pl.BlockSpec((BLK, PAIR), lambda i: (i, 0)),
            pl.BlockSpec((PAIR, 2 * length), lambda i: (0, 0)),
        ],
        out_shape=[
            jax.ShapeDtypeStruct((length, PAIR), BF16),
            jax.ShapeDtypeStruct((PAIR, 2 * length), BF16),
        ],
        scratch_shapes=[pltpu.VMEM((PAIR, 2 * length), F32)],
        compiler_params=pltpu.CompilerParams(vmem_limit_bytes=20 * 2**20),
        cost_estimate=pl.CostEstimate(
            flops=88 * length * length * PAIR, bytes_accessed=10 * 2**20, transcendentals=0
        ),
        name="attn_bwd_cols",
    )(k, qr, ds, qrev, *deps)


def to_16(rows):
    more = -rows.shape[0] % 16
    if more:
        rows = jnp.concatenate([rows, jnp.zeros((more, rows.shape[1]), rows.dtype)], axis=0)
    return rows


def up_16(count):
    return count + -count % 16


def pack_kernel(parts, at_ref, *refs):
    d_refs, g_refs = refs[:6], refs[6:10]
    hidden_ref, table_ref, rising_ref, falling_ref, vec_ref, out_ref = refs[10:]
    table_rows = table_ref.shape[0]
    length = rising_ref.shape[1]
    bucket = lax.broadcasted_iota(jnp.int32, (table_rows, length), 0)
    weights = []
    positions = []
    biases = []
    for which in range(3):
        d_both = jnp.concatenate([d_refs[2 * which][...], d_refs[2 * which + 1][...]], axis=1)
        grad = dot(d_both, hidden_ref[...], TN)
        bias = jnp.sum(d_both.astype(F32), axis=0, keepdims=True)
        if which < 2:
            index_ref = (rising_ref, falling_ref)[which]
            hot = (bucket == index_ref[...]).astype(F32).astype(BF16)
            rows = jnp.concatenate([g_refs[2 * which][...], g_refs[2 * which + 1][...]], axis=0)
            pos = dot(hot, rows, NT)
            bias = bias + jnp.sum(pos, axis=0, keepdims=True)
            grad = grad + dot(pos.astype(BF16), table_ref[...], TN)
            positions.append(pos)
        weights.append(grad)
        biases.append(bias)
    weights = jnp.concatenate(weights, axis=0)
    positions = jnp.concatenate(positions, axis=1)
    width = weights.shape[1]
    biases = jnp.concatenate(biases, axis=1)
    biases = jnp.concatenate([biases, jnp.zeros((1, width - biases.shape[1]), F32)], axis=1)
    mine = lax.broadcasted_iota(jnp.int32, (16, width), 0) == at_ref[0]
    vectors = vec_ref[...] + jnp.where(mine, biases, 0.0)
    step = weights.shape[0] // parts
    half = table_rows // parts // 2
    for b in range(parts):
        pos = positions[2 * b * half : 2 * (b + 1) * half]
        out_ref[b] = jnp.concatenate(
            [
                to_16(weights[b * step : (b + 1) * step]),
                to_16(jnp.concatenate([pos[:half], pos[half:]], axis=1)),
                vectors if b == 0 else jnp.zeros_like(vectors),
            ],
            axis=0,
        ).astype(BF16)


def pack(parts, at, d_parts, grads, hidden, table, rising, falling, vectors, deps=()):
    width = hidden.shape[1]
    cols = 6 * PAIR
    rows = up_16(cols // parts) + up_16(table.shape[0] // parts // 2) + 16
    return pl.pallas_call(
        ordered(functools.partial(pack_kernel, parts), 16, deps),
        in_specs=[pl.BlockSpec(memory_space=pltpu.SMEM)]
        + [pl.BlockSpec(memory_space=pltpu.VMEM)] * 15
        + [pl.BlockSpec(memory_space=pl.ANY)] * len(deps),
        out_specs=pl.BlockSpec(memory_space=pltpu.VMEM),
        out_shape=jax.ShapeDtypeStruct((parts, rows, width), BF16),
        compiler_params=pltpu.CompilerParams(vmem_limit_bytes=32 * 2**20),
        cost_estimate=pl.CostEstimate(flops=8 * 10**9, bytes_accessed=10 * 2**20, transcendentals=0),
        name="pack",
    )(at, *d_parts, *grads, hidden, table, rising, falling, vectors, *deps)


def unpack_kernel(step, table_step, in_ref, q_ref, k_ref, v_ref, table_ref, vec_ref):
    parts = in_ref.shape[0]
    rows = up_16(step)
    weights = jnp.concatenate([in_ref[b, :rows].astype(F32)[:step] for b in range(parts)], axis=0)
    width = q_ref.shape[1]
    for i, ref in enumerate((q_ref, k_ref, v_ref)):
        ref[...] = weights[i * width : (i + 1) * width].T
    table = [in_ref[b, rows : rows + up_16(table_step)].astype(F32)[:table_step] for b in range(parts)]
    table_ref[...] = jnp.concatenate(table, axis=0)
    vec_ref[...] = in_ref[0, rows + up_16(table_step) :].astype(F32)


def unpack(whole, cols, table_rows):
    parts, _, width = whole.shape
    weight = jax.ShapeDtypeStruct((width, cols), F32)
    return pl.pallas_call(
        functools.partial(unpack_kernel, 3 * cols // parts, table_rows // parts),
        in_specs=[pl.BlockSpec(memory_space=pltpu.VMEM)],
        out_specs=[pl.BlockSpec(memory_space=pltpu.VMEM)] * 5,
        out_shape=[weight] * 3
        + [jax.ShapeDtypeStruct((table_rows, width), F32), jax.ShapeDtypeStruct((16, width), F32)],
        compiler_params=pltpu.CompilerParams(vmem_limit_bytes=32 * 2**20),
        name="unpack",
    )(whole)


def widen_kernel(in_ref, *refs):
    rows = in_ref[0].astype(F32)
    start = 0
    for ref in refs:
        ref[...] = rows[start : start + ref.shape[0]]
        start += ref.shape[0]


def widen(gathered, counts):
    parts, rows, width = gathered.shape
    return pl.pallas_call(
        widen_kernel,
        grid=(parts,),
        in_specs=[pl.BlockSpec((1, rows, width), lambda b: (b, 0, 0))],
        out_specs=[pl.BlockSpec((count, width), lambda b: (b, 0)) for count in counts],
        out_shape=[jax.ShapeDtypeStruct((parts * count, width), F32) for count in counts],
        cost_estimate=pl.CostEstimate(flops=0, bytes_accessed=6 * parts * rows * width, transcendentals=0),
        name="widen",
    )(gathered)


def swap(values, axis, mask):
    return lax.ppermute(values, axis, [(i, i ^ mask) for i in range(lax.axis_size(axis))])


def after(value, *deps):
    return lax.optimization_barrier((value, *deps))[0]


def pick(values, index, axis=0):
    return lax.dynamic_index_in_dim(values, index, axis, keepdims=False)


def bit_of(axis, mask):
    return (lax.axis_index(axis) & mask) // mask


def add_low(left, right):
    return (left.astype(F32) + right.astype(F32)).astype(BF16)


def pick_bit(values, at, low, bit):
    shape = values.shape
    cut = values.reshape(shape[:at] + (shape[at] // (2 * low), 2, low) + shape[at + 1 :])
    part = pick(cut, bit, at + 1)
    return part.reshape(shape[:at] + (shape[at] // 2,) + shape[at + 1 :])


def send_together(arrays, axis, mask):
    last = arrays[0].shape[-1]
    got = swap(jnp.concatenate([a.reshape(-1, last) for a in arrays], axis=0), axis, mask)
    parts = []
    start = 0
    for a in arrays:
        rows = a.size // last
        parts.append(got[start : start + rows].reshape(a.shape))
        start += rows
    return parts


def halve(arrays, ats, low, mask):
    bit = bit_of("dp", mask)
    theirs = send_together([pick_bit(a, at, low, 1 - bit) for a, at in zip(arrays, ats)], "dp", mask)
    return [pick_bit(a, at, low, bit) for a, at in zip(arrays, ats)], theirs


def add_all(pair):
    return [add_low(mine, theirs) for mine, theirs in zip(*pair)]


def low_sum_over(values, axis, beside):
    mask = 1
    while mask < lax.axis_size(axis):
        values = add_low(values, swap(values, axis, mask))
        if mask == 1:
            values = after(values, beside)
        mask *= 2
    return values


def norm_parts(values):
    row_mean = jnp.mean(values, axis=-1, keepdims=True)
    centered = values - row_mean
    row_var = jnp.mean(centered * centered, axis=-1, keepdims=True)
    inverse = lax.rsqrt(row_var + NORM_EPS)
    return centered * inverse, inverse


def norm_back(grad, unit_rows, inverse, gain):
    d_unit = grad * gain
    mean_d = jnp.mean(d_unit, axis=-1, keepdims=True)
    mean_du = jnp.mean(d_unit * unit_rows, axis=-1, keepdims=True)
    return inverse * (d_unit - mean_d - unit_rows * mean_du)


def gelu_parts(values):
    cumulative = 0.5 + 0.5 * lax.erf(values * math.sqrt(0.5))
    density = jnp.exp(-0.5 * values * values) * (1.0 / math.sqrt(2.0 * math.pi))
    return values * cumulative, cumulative + values * density


def on_device(
    hidden_in,
    key_mask,
    bucket_of_offset,
    position_table,
    query_weight,
    query_bias,
    key_weight,
    key_bias,
    value_weight,
    value_bias,
    out_weight,
    out_bias,
    first_gain,
    first_shift,
    up_weight,
    up_bias,
    down_weight,
    down_bias,
    second_gain,
    second_shift,
    cotangent,
):
    tokens, width = hidden_in.shape
    width_loc = query_weight.shape[1]
    units = up_weight.shape[1]
    pairs = width_loc // PAIR
    dp_parts = lax.axis_size("dp")
    mp_parts = lax.axis_size("mp")
    dp_index = lax.axis_index("dp")
    mp_index = lax.axis_index("mp")
    share = tokens // mp_parts
    assert tokens == LEN and mp_parts == 4 and dp_parts & (dp_parts - 1) == 0
    dp_masks = [1 << b for b in range(dp_parts.bit_length() - 1)]
    others = range(1, mp_parts)

    def relative(blocks):
        return jnp.concatenate([pick(blocks, mp_index ^ s)[None] for s in range(mp_parts)], axis=0)

    def to_owners(blocks):
        return [blocks[0]] + [swap(blocks[s], "mp", s) for s in others]

    def by_owner(rows):
        blocks = rows.reshape(mp_parts, -1, rows.shape[1])
        return [pick(blocks, mp_index ^ s) for s in range(mp_parts)]

    def my_part(rows):
        count = rows.shape[0] // dp_parts
        return lax.dynamic_slice_in_dim(rows, dp_index * count, count, 0)

    out_slice = jnp.stack(to_owners([my_part(out_weight)] * mp_parts))
    bias_row = jnp.pad(up_bias.reshape(1, units), ((0, 15), (0, 0)))
    far_slice = jnp.concatenate([my_part(up_weight), my_part(down_weight), bias_row], axis=0)
    far_slice = swap(far_slice, "mp", 2)
    far_bias = far_slice[-16]

    row_two = (1, width_loc)
    falling = jnp.concatenate([bucket_of_offset[:1], bucket_of_offset[::-1]])[None, :]
    rising = jnp.concatenate([bucket_of_offset, bucket_of_offset[:1]])[None, :]
    queries, keys_all, values_all, key_rows, query_rows, query_rows_up = project(
        hidden_in,
        position_table,
        rising,
        falling,
        (query_weight, key_weight, value_weight),
        (query_bias.reshape(row_two), key_bias.reshape(row_two), value_bias.reshape(row_two)),
    )
    weight_cat = jnp.concatenate([query_weight, key_weight, value_weight], axis=1)

    out_all = jnp.swapaxes(lax.all_gather(out_slice, "dp", axis=0), 0, 1).reshape(width, width)

    probs, context = attn_fwd(
        queries, keys_all, values_all, key_rows, query_rows, key_mask.reshape(1, tokens)
    )
    far_all = lax.all_gather(after(far_slice, context), "dp", axis=0)
    ctx_rows = jnp.concatenate(to_owners(by_owner(context)), axis=1)

    own_rows = lax.dynamic_slice_in_dim(hidden_in, mp_index * share, share, 0)
    pre_first = dot(ctx_rows, out_all) + out_bias.astype(F32) + own_rows.astype(F32)
    unit_first, inverse_first = norm_parts(pre_first)
    gain_first = first_gain.astype(F32)
    normed = unit_first * gain_first + first_shift.astype(F32)
    normed_low = normed.astype(BF16)

    near_low = swap(normed_low, "mp", 1)
    up_cat = jnp.concatenate([up_weight, far_all[:, : width // dp_parts].reshape(width, units)], axis=1)
    down_cat = jnp.concatenate([down_weight, far_all[:, width // dp_parts : -16].reshape(units, width)], axis=0)
    bias_cat = jnp.concatenate([up_bias, far_bias], axis=0).astype(F32)

    def feed(rows):
        act, slope = gelu_parts(dot(rows, up_cat) + bias_cat)
        act_low = act.astype(BF16)
        return act_low, slope.astype(BF16), dot(act_low, down_cat)

    act_near, slope_near, mixed_near = feed(near_low)
    mixed_near = mixed_near.astype(BF16)
    act_own, slope_own, mixed_own = feed(after(normed_low, mixed_near))
    mixed = mixed_own + swap(mixed_near, "mp", 1).astype(F32)
    pre_second = mixed + down_bias.astype(F32) + normed

    unit_second, inverse_second = norm_parts(pre_second)
    gain_second = second_gain.astype(F32)
    layer_out = (unit_second * gain_second + second_shift.astype(F32)).astype(BF16)
    cot = cotangent.astype(F32)
    d_pre_second = norm_back(cot, unit_second, inverse_second, gain_second)
    d_down = d_pre_second.astype(BF16)

    near_d_down = swap(d_down, "mp", 1)

    def feed_back(d_rows, slope):
        d_inner = (dot(d_rows, down_cat, NT) * slope.astype(F32)).astype(BF16)
        return d_inner, dot(d_inner, up_cat, NT)

    d_inner_own, back_own = feed_back(d_down, slope_own)
    d_inner_near, back_near = feed_back(after(near_d_down, d_inner_own), slope_near)
    back_near = swap(back_near.astype(BF16), "mp", 1)
    d_normed = back_own + back_near.astype(F32) + d_pre_second
    act_cat = after(jnp.concatenate([act_own, act_near], axis=0), d_down)
    d_down_cat = jnp.concatenate([d_down, near_d_down], axis=0)
    normed_cat = after(jnp.concatenate([normed_low, near_low], axis=0), d_down)
    d_inner_cat = jnp.concatenate([d_inner_own, d_inner_near], axis=0)

    half = dp_parts // 2

    def blocks_of(cols, which, groups):
        step = cols.shape[1] // (groups * dp_parts)
        return jnp.concatenate(
            [
                lax.dynamic_slice_in_dim(cols, (g * dp_parts + 2 * j + which) * step, step, 1)
                for g in range(groups)
                for j in range(half)
            ],
            axis=1,
        )

    def halves_sum(make):
        bit = bit_of("dp", 1)
        theirs = swap(make(1 - bit).astype(BF16), "dp", 1)
        return (make(bit) + theirs.astype(F32)).astype(BF16)

    down_sum = halves_sum(lambda which: dot(blocks_of(act_cat, which, 2), d_down_cat, TN))
    down_sum = down_sum.reshape(2, half, units // dp_parts, width)
    up_sum = halves_sum(lambda which: dot(blocks_of(normed_cat, which, 1), d_inner_cat, TN))
    up_sum = up_sum.reshape(half, width // dp_parts, 2 * units)
    up_bias_part = jnp.sum(d_inner_cat.astype(F32), axis=0)

    d_pre_first = norm_back(d_normed, unit_first, inverse_first, gain_first)
    d_attn = d_pre_first.astype(BF16)
    d_ctx = dot(d_attn, out_all, NT).astype(BF16)
    d_ctx_parts = jnp.stack(
        to_owners([d_ctx[:, s * width_loc : (s + 1) * width_loc] for s in range(mp_parts)])
    )
    out_sum = dot(ctx_rows, d_attn, TN).astype(BF16).reshape(mp_parts, dp_parts, -1, width)
    sums = jnp.stack(
        [
            jnp.sum(d_pre_first, axis=0),
            jnp.sum(d_normed * unit_first, axis=0),
            jnp.sum(d_normed, axis=0),
            jnp.sum(d_pre_second, axis=0),
            jnp.sum(cot * unit_second, axis=0),
            jnp.sum(cot, axis=0),
        ]
    )

    d_ctx = jnp.concatenate(
        [pick(d_ctx_parts, mp_index ^ s) for s in range(mp_parts)], axis=0
    )

    def rows_step(pair, deps):
        return attn_bwd_rows(pair, queries, keys_all, values_all, key_rows, probs, d_ctx, deps)

    def cols_step(pair, deps):
        _, _, _, d_score, turned = by_rows[pair]
        return attn_bwd_cols(pair, keys_all, query_rows_up, d_score, turned, deps)

    low_bits = list(range(len(dp_masks) - 1))
    cut = max(1, len(low_bits) // 2)

    def steps(arrays, ats, bits, left):
        pair = None
        for bit in bits:
            pair = halve(arrays if pair is None else add_all(pair), ats, 1 << left.index(bit), 2 << bit)
            left.remove(bit)
        return pair

    def tied(pair, *deps):
        return pair[0], [after(theirs, *deps) for theirs in pair[1]]

    left_one, left_two = list(low_bits), list(low_bits)
    bits_one, bits_two = low_bits, low_bits[::-1]
    step_two = steps([up_sum], [0], bits_two[:cut], left_two)
    step_out = halve([out_sum], [1], 1, 1)
    step_one = steps([down_sum], [1], bits_one[:cut], left_one)
    by_rows = [rows_step(0, (up_sum, down_sum, step_out[0][0]))]
    (down_sum,) = add_all(tied(step_one, by_rows[0][1]))
    (up_sum,) = add_all(tied(step_two, by_rows[0][1]))
    (out_sum,) = add_all(tied(step_out, by_rows[0][1]))
    step_one = steps([down_sum], [1], bits_one[cut:], left_one)
    step_two = steps([up_sum], [0], bits_two[cut:], left_two)
    step_out = steps([out_sum], [1], bits_one[:cut], list(low_bits))
    by_rows.append(rows_step(1, (by_rows[0][1], down_sum, up_sum, out_sum)))
    d_query, d_value = (jnp.concatenate([r[i] for r in by_rows], axis=1) for i in (0, 1))
    key_grad = jnp.concatenate([r[2] for r in by_rows], axis=0)
    d_value1 = by_rows[1][1]
    (down_sum,) = add_all(tied(step_one, d_value1))
    (up_sum,) = add_all(tied(step_two, d_value1))
    (out_sum,) = add_all(tied(step_out, d_value1))
    step_out = steps([out_sum], [1], bits_one[cut:], low_bits[cut:])
    down_sum, up_sum = down_sum[:, 0], up_sum[0]
    down_rows = down_sum.shape[1]
    far = send_together([down_sum[1], up_sum[:, units:]], "mp", 2)
    by_cols = [cols_step(0, (down_sum, up_sum, out_sum))]
    (out_sum,) = add_all(tied(step_out, by_cols[0][0]))
    out_sum = out_sum[:, 0]
    out_rows = out_sum.shape[1]
    by_cols.append(cols_step(1, (by_cols[0][0], out_sum)))
    d_key = jnp.concatenate([r[0] for r in by_cols], axis=1)
    query_grad = jnp.concatenate([r[1] for r in by_cols], axis=0)
    out_parts = to_owners([out_sum[s] for s in range(mp_parts)])
    out_sum = out_parts[0].astype(F32) + sum(after(p, d_key).astype(F32) for p in out_parts[1:])
    far = [after(part, d_key) for part in far]
    ready = jnp.concatenate(
        [
            add_low(down_sum[0], far[0]),
            add_low(up_sum[:, :units], far[1]),
            out_sum.astype(BF16),
        ],
        axis=0,
    )
    gathered = lax.all_gather(ready, "dp", axis=0)
    d_key1 = after(by_cols[1][0], ready)

    device_ids = jnp.arange(mp_parts)[:, None]
    up_bias_part = jnp.where(device_ids == mp_index, up_bias_part[:units], 0.0) + jnp.where(
        device_ids == (mp_index ^ 2), up_bias_part[units:], 0.0
    )
    vectors = jnp.concatenate([jnp.zeros_like(up_bias_part), sums, up_bias_part], axis=0)
    vectors = jnp.pad(vectors, ((0, 16 - vectors.shape[0]), (0, 0)))
    message = pack(
        dp_parts,
        mp_index.reshape(1),
        [by_rows[0][0], by_rows[1][0], by_cols[0][0], d_key1, by_rows[0][1], by_rows[1][1]],
        [by_cols[0][1], by_cols[1][1], by_rows[0][2], by_rows[1][2]],
        hidden_in,
        position_table,
        rising,
        falling,
        vectors,
    )

    d_cat = after(jnp.concatenate([d_query, d_key, d_value], axis=1), message)
    input_low = dot(d_cat, weight_cat, NT).astype(BF16)
    (message,) = add_all(halve([message], [0], 1, 1))
    block_index = dp_index // 2

    def sum_chips(rows):
        total = pick(rows, block_index).astype(F32)
        for s in range(1, half):
            total = total + swap(pick(rows, block_index ^ s), "dp", 2 * s).astype(F32)
        return total

    down_weight_grad, up_weight_grad, out_weight_grad = widen(gathered, (down_rows, down_rows, out_rows))
    step = 3 * width_loc // dp_parts
    short = sum_chips(message[:, up_16(step) :])
    weights_sum = sum_chips(message[:, : up_16(step)]).astype(BF16)
    table_rows = position_table.shape[0]
    table_step = table_rows // dp_parts
    packed = short[: table_step // 2].astype(BF16)
    packed = jnp.concatenate([packed[:, : 2 * width_loc], packed[:, 2 * width_loc :]], axis=0)
    table_part = dot(packed, weight_cat[:, : 2 * width_loc], NT)
    shared_sum = jnp.concatenate([to_16(table_part), short[-16:]], axis=0).astype(BF16)
    shared_sum = low_sum_over(shared_sum, "mp", weights_sum)
    block = jnp.concatenate([weights_sum, shared_sum], axis=0)
    input_part = lax.psum_scatter(after(input_low, gathered, shared_sum), "mp", scatter_dimension=0, tiled=True)
    input_grad = d_pre_first + input_part.astype(F32)

    parts = jnp.stack([block] + [swap(block, "dp", 2 * s) for s in range(1, half)])
    mine = jnp.stack([pick(parts, block_index ^ j) for j in range(half)])
    theirs = swap(mine, "dp", 1)
    even = bit_of("dp", 1) == 0
    whole = jnp.stack([jnp.where(even, mine, theirs), jnp.where(even, theirs, mine)], axis=1)
    whole = whole.reshape(dp_parts, -1, width)
    query_weight_grad, key_weight_grad, value_weight_grad, table_grad, vectors = unpack(
        whole, width_loc, table_rows
    )
    biases = lax.dynamic_index_in_dim(vectors, mp_index, 0, keepdims=False)
    query_bias_grad, key_bias_grad, value_bias_grad = (
        biases[i * width_loc : (i + 1) * width_loc] for i in range(3)
    )
    shared_sums = vectors[mp_parts:]
    up_bias_grad = lax.dynamic_index_in_dim(vectors, mp_parts + 6 + mp_index, 0, keepdims=False)

    out_bias_grad, first_gain_grad, first_shift_grad, down_bias_grad, second_gain_grad, second_shift_grad = (
        shared_sums[i] for i in range(6)
    )
    return (
        layer_out,
        input_grad,
        table_grad,
        query_weight_grad,
        query_bias_grad,
        key_weight_grad,
        key_bias_grad,
        value_weight_grad,
        value_bias_grad,
        out_weight_grad,
        out_bias_grad,
        first_gain_grad,
        first_shift_grad,
        up_weight_grad,
        up_bias_grad,
        down_weight_grad,
        down_bias_grad,
        second_gain_grad,
        second_shift_grad,
    )


def solution(mesh):
    return jax.shard_map(
        on_device,
        mesh=mesh,
        in_specs=(
            P("dp", None),
            P("dp"),
            P(),
            P(),
            P(None, "mp"),
            P("mp"),
            P(None, "mp"),
            P("mp"),
            P(None, "mp"),
            P("mp"),
            P("mp", None),
            P(),
            P(),
            P(),
            P(None, "mp"),
            P("mp"),
            P("mp", None),
            P(),
            P(),
            P(),
            P(("dp", "mp"), None),
        ),
        out_specs=(
            P(("dp", "mp"), None),
            P(("dp", "mp"), None),
            P(),
            P(None, "mp"),
            P("mp"),
            P(None, "mp"),
            P("mp"),
            P(None, "mp"),
            P("mp"),
            P("mp", None),
            P(),
            P(),
            P(),
            P(None, "mp"),
            P("mp"),
            P("mp", None),
            P(),
            P(),
            P(),
        ),
        check_vma=False,
    )
```
